32 devices in a mesh: gx: 4 (over z), gy: 8 (over y, x, core).
Axes of the slice: x: 2, y: 2, z: 4, core: 2. Of those that a mesh axis runs over, the one named last changes fastest.
Arguments:
- feats: bfloat16 [96, 4, 128, 512], P(None, 'gx', 'gy'), may hold values from -6 to 6
- cotangent: bfloat16 [96, 4, 128, 512], P(None, 'gx', 'gy'), may hold values from -6 to 6
- weight: bfloat16 [96, 2592], replicated, may hold values from -0.125 to 0.125
- cell_slot: int32 [4, 288], P('gx', 'gy'), may hold values from 0 to 16, as said below
- neighbours: int32 [4, 128, 8], P('gx', 'gy'), may hold values from 0 to 44, as said below
- counts: int32 [4, 8], P('gx', 'gy'), may hold values from 2 to 16, as said below
Outputs:
- output: bfloat16 [96, 4, 128, 512], P(None, 'gx', 'gy')
- grad_feats: bfloat16 [96, 4, 128, 512], P(None, 'gx', 'gy')
- grad_weight: float32 [96, 2592], replicated
The draws below stay inside these ranges and needn't reach their ends.
Inputs may be any that keep to these rules, and one draw needn't show every extreme that they name: `cell_slot`: on each device the live slots are 0 to counts-1, each sits at exactly one tile position, in increasing order of position a*6+b; empty positions hold 16; some device has all 16 slots live. neighbours[i, j, s, k] is the source-table index of the live brick at the city position one step in direction k from slot s, or 45 - 1 (the zero brick) where no live brick is there or s is not live. Neighbours in the same tile are given by their slot; the others by their halo entry. `counts`: devices differ in load; the busiest holds 16 live bricks.
All inputs are finite; a program needn't handle non-finite values.
Results may differ from the reference program's by a relative error of at most 0.0022.
The reference program's roundings to bfloat16 on the way count: a program that leaves them out, or rounds other values in their place, can miss the bound.
Values may be sent and summed in bfloat16 or wider, within the bound.
No kernel may reach another device: no remote copies, remote signals or barrier semaphores. Data moves between devices by JAX's collectives and lax.ppermute only.
A program may use at most 128 MiB of HBM per device.

```python
import math
import jax
import jax.numpy as jnp
from jax import lax

C = 96
VOX = 512
TILE = 6
CAP = 16
NSRC = 45
TOTAL_VOX = 262144
N_GX = 4
N_GY = 8


DIRECTIONS = ((-1, -1), (-1, 0), (-1, 1), (0, -1), (0, 1), (1, -1), (1, 0), (1, 1))


def city_layout(key):
    device_total = N_GX * N_GY
    key_rank, key_level, key_place = jax.random.split(key, 3)
    device_ids = jnp.arange(device_total, dtype=jnp.int32)
    device_x = device_ids // N_GY
    device_y = device_ids % N_GY
    levels = jax.random.randint(key_level, (device_total,), 0, 4).astype(jnp.int32)
    levels = jnp.where(device_y == 0, 0, jnp.where((device_y == 1) & (device_x == 0), 3, levels)).astype(jnp.int32)
    full_cap = jnp.full((device_total,), CAP, jnp.int32)
    live_counts = jnp.maximum(jnp.right_shift(full_cap, levels), 1).astype(jnp.int32)
    places = TILE * TILE
    place_keys = jax.random.split(key_place, device_total)
    scores = jax.vmap(lambda single: jax.random.permutation(single, places))(place_keys).astype(jnp.int32)
    place_ids = jnp.arange(places, dtype=jnp.int32)[None, :]
    first_edge = place_ids == 0
    second_edge = place_ids == (TILE - 1) * TILE
    special = first_edge | second_edge
    score_first = scores[:, 0:1]
    score_second = scores[:, (TILE - 1) * TILE:(TILE - 1) * TILE + 1]
    adjusted = scores - (score_first < scores).astype(jnp.int32) - (score_second < scores).astype(jnp.int32)
    edge_device = (device_y == 0)[:, None]
    occupied_edge = special | ~special & (adjusted < live_counts[:, None] - 2)
    occupied_plain = scores < live_counts[:, None]
    occupied = jnp.where(edge_device, occupied_edge, occupied_plain)
    slot_ids = jnp.cumsum(occupied.astype(jnp.int32), axis=1) - 1
    cell_table = jnp.where(occupied, slot_ids, CAP).astype(jnp.int32)
    city_map = cell_table.reshape(N_GX, N_GY, TILE, TILE).transpose(0, 2, 1, 3).reshape(N_GX * TILE, N_GY * TILE)
    slot_range = jnp.arange(CAP, dtype=jnp.int32)
    matches = cell_table[:, None, :] == slot_range[None, :, None]
    position = jnp.sum(jnp.where(matches, jnp.arange(places, dtype=jnp.int32)[None, None, :], 0), axis=2).astype(jnp.int32)
    live = slot_range[None, :] < live_counts[:, None]
    brick_x = position // TILE
    brick_y = position % TILE
    entries = []
    for step_x, step_y in DIRECTIONS:
        near_x = brick_x + step_x
        near_y = brick_y + step_y
        city_x = (device_x[:, None] * TILE + near_x) % (N_GX * TILE)
        city_y = device_y[:, None] * TILE + near_y
        inside_y = (city_y >= 0) & (city_y < N_GY * TILE)
        found = city_map[city_x, jnp.clip(city_y, 0, N_GY * TILE - 1)]
        present = inside_y & (found < CAP) & live
        tile_x = (near_x >= 0) & (near_x < TILE)
        tile_y = (near_y >= 0) & (near_y < TILE)
        halo_index = jnp.where(tile_y, jnp.where(near_x < 0, CAP + near_y, CAP + TILE + near_y), jnp.where(near_y < 0, CAP + 2 * TILE + near_x + 1, CAP + 3 * TILE + 2 + near_x + 1))
        source_index = jnp.where(tile_x & tile_y, found, halo_index)
        entries.append(jnp.where(present, source_index, CAP + 4 * TILE + 4).astype(jnp.int32))
    neighbour_ids = jnp.stack(entries, axis=-1)
    return (live_counts, cell_table, neighbour_ids)


def draw_cell_slot(key, part):
    live_counts, cell_table, neighbour_ids = city_layout(jax.random.fold_in(key, 5))
    return cell_table.reshape(N_GX, N_GY * TILE * TILE).astype(jnp.int32)


def draw_neighbours(key, part):
    live_counts, cell_table, neighbour_ids = city_layout(jax.random.fold_in(key, 5))
    return neighbour_ids.reshape(N_GX, N_GY * CAP, 8).astype(jnp.int32)


def draw_counts(key, part):
    live_counts, cell_table, neighbour_ids = city_layout(jax.random.fold_in(key, 5))
    return live_counts.reshape(N_GX, N_GY).astype(jnp.int32)


def level_of(key, dims, pieces, smallest, largest):
    gain = 1.0
    for axis_at, blocks in pieces:
        heights = jax.random.uniform(jax.random.fold_in(jax.random.fold_in(key, 6), axis_at), (blocks,), jnp.float32, smallest / len(pieces), largest / len(pieces))
        gain = gain * jnp.repeat(jnp.exp(heights), dims[axis_at] // blocks).reshape((-1,) + (1,) * (len(dims) - 1 - axis_at))
    return gain


def centred(stream_key, shape, scale, bound, pieces=(), kind=jnp.bfloat16):
    values = scale * jax.random.normal(stream_key, shape, jnp.float32)
    if pieces:
        values = values * level_of(stream_key, shape, pieces, -0.22, 0.18)
    return jnp.clip(values, -bound, bound).astype(kind)


def setup_inputs(seed: int = 0) -> dict:
    splits = jax.random.split(jax.random.key(seed), 7)
    feats = centred(splits[0], (C, N_GX, N_GY * CAP, VOX), 1.0, 6.0, ((1, 4), (2, 8)))
    cotangent = centred(splits[1], (C, N_GX, N_GY * CAP, VOX), 1.0, 6.0, ((1, 4), (2, 8)))
    weight = centred(splits[2], (C, 27 * C), (27 * C) ** -0.5, 0.125)
    cell_slot = draw_cell_slot(jax.random.fold_in(splits[6], 71), 0)
    neighbours = draw_neighbours(jax.random.fold_in(splits[6], 71), 0)
    counts = draw_counts(jax.random.fold_in(splits[6], 71), 0)
    return {"feats": feats, "cotangent": cotangent, "weight": weight, "cell_slot": cell_slot, "neighbours": neighbours, "counts": counts}


DIRECTIONS = ((-1, -1), (-1, 0), (-1, 1), (0, -1), (0, 1), (1, -1), (1, 0), (1, 1))

def extent(step):
    if step < 0:
        return (7, 8)
    if step == 0:
        return (0, 8)
    return (0, 1)

def trim_region(region, step_x, step_y):
    low_x, high_x = extent(step_x)
    low_y, high_y = extent(step_y)
    piece = region if region.shape[2] == 1 else region[:, :, low_x:high_x]
    piece = piece if piece.shape[3] == 1 else piece[:, :, :, low_y:high_y]
    return jnp.broadcast_to(piece, piece.shape[:2] + (high_x - low_x, high_y - low_y, piece.shape[4]))

def assemble(regions, links, center):
    x_layers = []
    for step_x in (-1, 0, 1):
        y_pieces = []
        for step_y in (-1, 0, 1):
            if step_x == 0 and step_y == 0:
                y_pieces.append(center)
            else:
                direction = DIRECTIONS.index((step_x, step_y))
                sources = jnp.concatenate([trim_region(region, step_x, step_y) for region in regions], axis=1)
                y_pieces.append(jnp.take(sources, links[:, direction], axis=1))
        x_layers.append(jnp.concatenate(y_pieces, axis=3))
    filled = jnp.concatenate(x_layers, axis=2)
    return jnp.pad(filled, ((0, 0), (0, 0), (0, 0), (0, 0), (1, 1)))

def convolve(padded, matrix):
    channels = padded.shape[0]
    slot_count = padded.shape[1]
    summed = jnp.zeros((matrix.shape[0], slot_count * 512), jnp.float32)
    for offset_x in range(3):
        for offset_y in range(3):
            stacked = jnp.concatenate([padded[:, :, offset_x:offset_x + 8, offset_y:offset_y + 8, offset_z:offset_z + 8].reshape(channels, slot_count * 512) for offset_z in range(3)], axis=0)
            column_start = (offset_x * 3 + offset_y) * 3 * channels
            summed = summed + jnp.dot(matrix[:, column_start:column_start + 3 * channels], stacked, preferred_element_type=jnp.float32)
    return summed

def weight_terms(padded, grad_rows):
    channels = padded.shape[0]
    slot_count = padded.shape[1]
    blocks = []
    for offset_x in range(3):
        for offset_y in range(3):
            stacked = jnp.concatenate([padded[:, :, offset_x:offset_x + 8, offset_y:offset_y + 8, offset_z:offset_z + 8].reshape(channels, slot_count * 512) for offset_z in range(3)], axis=0)
            blocks.append(lax.dot_general(grad_rows, stacked, (((1,), (1,)), ((), ())), preferred_element_type=jnp.float32))
    return jnp.concatenate(blocks, axis=1)

def surround(global_bricks, cells, links, row, column):
    along = jnp.arange(TILE, dtype=jnp.int32)
    wide = jnp.arange(TILE + 2, dtype=jnp.int32)
    base_t = jnp.zeros((TILE,), jnp.int32)
    base_u = jnp.zeros((TILE + 2,), jnp.int32)
    corner_x = (row * TILE + wide - 1) // TILE % N_GX
    source_x = jnp.concatenate([base_t + (row - 1) % N_GX, base_t + (row + 1) % N_GX, corner_x, corner_x])
    source_y = jnp.concatenate([base_t + column, base_t + column, base_u + column - 1, base_u + column + 1])
    cell_x = jnp.concatenate([base_t + TILE - 1, base_t, (wide - 1) % TILE, (wide - 1) % TILE])
    cell_y = jnp.concatenate([along, along, base_u + TILE - 1, base_u])
    inside = (source_y >= 0) & (source_y < N_GY)
    safe_y = jnp.clip(source_y, 0, N_GY - 1).astype(jnp.int32)
    slot_ids = cells[source_x, safe_y, cell_x, cell_y]
    present = inside & (slot_ids < CAP)
    halo_bricks = global_bricks[:, source_x, safe_y, jnp.minimum(slot_ids, CAP - 1)]
    halo_bricks = jnp.where(present[None, :, None], halo_bricks, jnp.zeros((), global_bricks.dtype))
    center = global_bricks[:, row, column]
    blank = jnp.zeros((C, 1, VOX), global_bricks.dtype)
    sources = jnp.concatenate([center, halo_bricks, blank], axis=1).reshape(C, NSRC, 8, 8, 8)
    return assemble((sources,), links[row, column], center.reshape(C, CAP, 8, 8, 8))

def reference(feats, cotangent, weight, cell_slot, neighbours, counts):
    grid_feats = feats.reshape(C, N_GX, N_GY, CAP, VOX)
    grid_upstream = cotangent.reshape(C, N_GX, N_GY, CAP, VOX)
    cells = cell_slot.reshape(N_GX, N_GY, TILE, TILE)
    links = neighbours.reshape(N_GX, N_GY, CAP, 8)
    live_all = jnp.arange(CAP, dtype=jnp.int32)[None, None, :] < counts[:, :, None]
    device_ids = jnp.arange(N_GX * N_GY, dtype=jnp.int32)

    def forward(index):
        row = index // N_GY
        column = index % N_GY
        padded = surround(grid_feats, cells, links, row, column)
        hidden = convolve(padded, weight).reshape(C, CAP, VOX)
        gate = jax.nn.sigmoid(hidden)
        live = live_all[row, column][None, :, None]
        inputs = grid_feats[:, row, column].astype(jnp.float32)
        upstream = grid_upstream[:, row, column].astype(jnp.float32)
        output = jnp.where(live, inputs + hidden * gate, 0.0).astype(jnp.bfloat16)
        grad_hidden = jnp.where(live, upstream * gate * (1.0 + hidden * (1.0 - gate)), 0.0).astype(jnp.bfloat16)
        return (output, grad_hidden)
    outputs, grad_hidden = lax.map(forward, device_ids)
    grid_grad = grad_hidden.reshape(N_GX, N_GY, C, CAP, VOX).transpose(2, 0, 1, 3, 4)
    flipped = weight.reshape(C, 27, C)[:, ::-1, :].transpose(2, 1, 0).reshape(C, 27 * C)

    def backward(summed, index):
        row = index // N_GY
        column = index % N_GY
        padded = surround(grid_feats, cells, links, row, column)
        padded_grad = surround(grid_grad, cells, links, row, column)
        back = convolve(padded_grad, flipped).reshape(C, CAP, VOX)
        live = live_all[row, column][None, :, None]
        upstream = grid_upstream[:, row, column].astype(jnp.float32)
        grad_feats = jnp.where(live, upstream + back, 0.0).astype(jnp.bfloat16)
        terms = weight_terms(padded, grid_grad[:, row, column].reshape(C, CAP * VOX))
        return (summed + terms, grad_feats)
    initial = jnp.zeros((C, 27 * C), jnp.float32)
    summed, grad_all = lax.scan(backward, initial, device_ids)
    grad_weight = summed * (1.0 / math.sqrt(TOTAL_VOX))

    def arrange(stacked):
        return stacked.reshape(N_GX, N_GY, C, CAP, VOX).transpose(2, 0, 1, 3, 4).reshape(C, N_GX, N_GY * CAP, VOX)
    return (arrange(outputs), arrange(grad_all), grad_weight)
```

```python
import functools
import math

import jax
import jax.numpy as jnp
from jax import lax
from jax.experimental import pallas as pl
from jax.experimental.pallas import tpu as pltpu
from jax.sharding import PartitionSpec as P

BF = jnp.bfloat16
F32 = jnp.float32
VMEM = pl.BlockSpec(memory_space=pltpu.VMEM)
SMEM = pl.BlockSpec(memory_space=pltpu.SMEM)
LANES = 128
HALF = 64
ROWS = 2048


def passed_along(block, axis, distance):
    devices = range(lax.axis_size(axis))
    route = [((i - distance) % len(devices), i) for i in devices]
    return lax.ppermute(block, axis, route)


def from_behind(block, axis, distance):
    devices = range(lax.axis_size(axis))
    route = [(i - distance, i) for i in devices if i - distance in devices]
    return lax.ppermute(block, axis, route)


def lane_ids(channels):
    return lax.broadcasted_iota(jnp.int32, (channels, LANES), 1)


def turn(value, amount):
    return pltpu.roll(value, amount, 1)


def nothing(value):
    return jnp.zeros_like(value)


def load_pairs(source, staging, target):
    channels, slots, _ = source.shape
    low = lane_ids(channels) < HALF
    for tile in range(4):
        piece = source[:, :, tile * LANES : (tile + 1) * LANES].astype(F32)
        staging[tile] = piece.reshape(channels * slots, LANES)

    def body(pair, carry):
        for tile in range(4):
            first = staging[tile, pl.ds(2 * pair, channels, stride=slots), :].astype(BF)
            second = staging[tile, pl.ds(2 * pair + 1, channels, stride=slots), :].astype(BF)
            target[pair, 2 * tile] = jnp.where(low, first, turn(second, HALF))
            target[pair, 2 * tile + 1] = jnp.where(low, turn(first, HALF), second)
        return carry

    lax.fori_loop(0, slots // 2, body, 0)


def edge_rows(cells, field, low_out, high_out, slots, side):
    channels = field.shape[2]
    low = lane_ids(channels) < HALF
    for out, line, layer in ((low_out, 0, 0), (high_out, side - 1, 7)):
        for tile in range(side // 2):
            parts = []
            for part in range(2):
                slot = cells[line * side + 2 * tile + part]
                row = field[jnp.minimum(slot, slots - 1) // 2, layer]
                row = turn(row, (part + slot) % 2 * HALF)
                parts.append(jnp.where(slot < slots, row, nothing(row)))
            out[tile] = jnp.where(low, parts[0], parts[1])


def prepare_kernel(cells, feats, pairs, low_out, high_out, staging, *, side):
    load_pairs(feats, staging, pairs)
    edge_rows(cells, pairs, low_out, high_out, feats.shape[1], side)


def regroup_kernel(source, pairs, staging):
    load_pairs(source, staging, pairs)


def column_kernel(cells, field, below, above, low_out, high_out, *, side):
    channels = field.shape[2]
    slots = 2 * field.shape[0]
    lanes = lane_ids(channels)
    for out, line, place in ((low_out, 0, 0), (high_out, side - 1, 56)):
        corner = line % 2 * HALF + place
        for quarter in range(4):
            total = jnp.zeros((channels, LANES), BF)
            for half in range(2):
                layer = quarter + 4 * half
                for u in range(1, side + 1):
                    slot = cells[(u - 1) * side + line]
                    row = field[jnp.minimum(slot, slots - 1) // 2, layer]
                    goal = half * HALF + u * 8
                    row = turn(row, (goal - place + LANES - slot % 2 * HALF) % LANES)
                    row = jnp.where(slot < slots, row, nothing(row))
                    total = jnp.where(lanes // 8 == goal // 8, row, total)
                if layer == 7:
                    goal = half * HALF
                    row = turn(below[line // 2], (goal - corner) % LANES)
                    total = jnp.where(lanes // 8 == goal // 8, row, total)
                if layer == 0:
                    goal = half * HALF + (side + 1) * 8
                    row = turn(above[line // 2], (goal - corner) % LANES)
                    total = jnp.where(lanes // 8 == goal // 8, row, total)
            out[quarter] = total


def fill_table(table, field, below_x, above_x, below_y, above_y):
    pairs, _, channels, _ = field.shape
    low = lane_ids(channels) < HALF

    def body(pair, carry):
        table[pair] = field[pair]
        return carry

    lax.fori_loop(0, pairs, body, 0)
    for quarter in range(4):
        below, above = below_y[quarter], above_y[quarter]
        table[pairs, quarter] = jnp.where(low, below, turn(above, HALF))
        table[pairs, quarter + 4] = jnp.where(low, turn(below, HALF), above)
    tiles = below_x.shape[0]
    for tile in range(tiles):
        table[pairs + 1 + tile, 7] = below_x[tile]
        table[pairs + 1 + tile, 0] = above_x[tile]
    table[pairs + 1 + tiles] = jnp.zeros(table.shape[1:], BF)


def locate(index, pairs, side, column):
    slots = 2 * pairs
    tiles = side // 2
    wide = side + 2
    place = 0 if column is None else column * 8
    own = index < slots
    row = index < slots + 2 * side
    below = index < slots + side
    ordinal = jnp.where(own, index, index - slots - jnp.where(below, 0, side))
    base = jnp.where(own, 0, pairs + 1)
    tile_row = base + ordinal // 2
    lane_row = ordinal % 2 * HALF + place
    last = index >= slots + 2 * side + 2 * wide
    u = index - slots - 2 * side
    lane_column = jnp.where(u < wide, u * 8, HALF + (u - wide) * 8)
    tile = jnp.where(row, tile_row, jnp.where(last, pairs + 1 + tiles, pairs))
    lane = jnp.where(row, lane_row, jnp.where(last, 0, lane_column))
    return tile, lane


def build_columns(group, links, table, columns, pairs, side):
    channels = table.shape[2]
    lanes = lane_ids(channels)
    low = lanes < HALF
    y_first = lanes % HALF < 8
    y_last = lanes % HALF >= 56
    z_first = lanes % 8 == 0
    z_last = lanes % 8 == 7
    spots = {}
    for h in range(2):
        for part in range(2):
            slot = group * 4 + 2 * h + part
            for k, (dx, dy) in enumerate(
                ((-1, -1), (-1, 0), (-1, 1), (0, -1), (0, 1), (1, -1), (1, 0), (1, 1))
            ):
                column = {-1: 7, 0: None, 1: 0}[dy]
                goal = part * HALF + (56 if dy == 1 else 0)
                tile, lane = locate(links[slot * 8 + k], pairs, side, column)
                spots[h, part, dx, dy] = tile, (goal + LANES - lane) % LANES

    def fetch(layer, h, dx, dy):
        rows = []
        for part in range(2):
            tile, amount = spots[h, part, dx, dy]
            rows.append(turn(table[tile, layer], amount))
        return jnp.where(low, rows[0], rows[1])

    def layer_of(xp, layer, dx):
        for h in range(2):
            if dx == 0:
                middle = table[group * 2 + h, layer]
            else:
                middle = fetch(layer, h, dx, 0)
            before = jnp.where(y_first, fetch(layer, h, dx, -1), turn(middle, 8))
            after = jnp.where(y_last, fetch(layer, h, dx, 1), turn(middle, LANES - 8))
            at = pl.multiple_of(xp * 2 * LANES + h * LANES, LANES)
            for b, value in enumerate((before, middle, after)):
                lower = jnp.where(z_first, nothing(value), turn(value, 1))
                upper = jnp.where(z_last, nothing(value), turn(value, LANES - 1))
                for c, shifted in enumerate((lower, value, upper)):
                    start = (b * 3 + c) * channels
                    columns[start : start + channels, pl.ds(at, LANES)] = shifted

    layer_of(0, 7, -1)

    def body(xp, carry):
        layer_of(xp, xp - 1, 0)
        return carry

    lax.fori_loop(1, 9, body, 0)
    layer_of(9, 0, 1)


def product(left, right, contract):
    return lax.dot_general(left, right, (contract, ((), ())), preferred_element_type=F32)


def convolve_group(matrix, columns, carry_ref, finish):
    channels = matrix.shape[0] // 3
    width = 2 * LANES
    for step in range(5):
        part = product(
            matrix[...], columns[:, step * 2 * width : (step + 1) * 2 * width], ((1,), (0,))
        )
        first, second, third = (part[a * channels : (a + 1) * channels] for a in range(3))
        if step > 0:
            left = carry_ref[:, :width] + third[:, :width]
            right = carry_ref[:, width:] + (second[:, :width] + third[:, width:])
            finish(step - 1, left, right)
        if step < 4:
            carry_ref[:, :width] = first[:, :width] + second[:, width:]
            carry_ref[:, width:] = first[:, width:]


def store_slots(staging, t, pair, slots, even, odd):
    channels = even.shape[0]
    low = lane_ids(channels) < HALF
    first = jnp.where(low, even, turn(odd, HALF))
    second = jnp.where(low, turn(even, HALF), odd)
    staging[t, pl.ds(2 * pair, channels, stride=slots), :] = first.astype(F32)
    staging[t, pl.ds(2 * pair + 1, channels, stride=slots), :] = second.astype(F32)


def write_out(staging, out):
    channels, slots, _ = out.shape
    for tile in range(4):
        out[:, :, tile * LANES : (tile + 1) * LANES] = (
            staging[tile].reshape(channels, slots, LANES).astype(BF)
        )


def forward_kernel(
    cells, links, counts, field, below_x, above_x, below_y, above_y, upstream, matrix,
    out, grad, terms, low_out, high_out,
    table, columns, shifted, carry_ref, total, staging, *, side,
):
    pairs, _, channels, _ = field.shape
    slots = 2 * pairs
    fill_table(table, field, below_x, above_x, below_y, above_y)
    total[...] = jnp.zeros(total.shape, F32)
    shifted[...] = jnp.zeros(shifted.shape, BF)
    upper = (lane_ids(channels) >= HALF).astype(jnp.int32)

    def body(group, carry):
        build_columns(group, links, table, columns, pairs, side)

        def finish(t, left, right):
            for h in range(2):
                pair = group * 2 + h
                live = 2 * pair + upper < counts[0]
                results = []
                for odd, hidden in ((0, left), (1, right)):
                    x = 2 * t + odd
                    hidden = hidden[:, h * LANES : (h + 1) * LANES]
                    gate = jax.nn.sigmoid(hidden)
                    inputs = field[pair, x].astype(F32)
                    gradient = upstream[pair, x].astype(F32)
                    result = jnp.where(live, inputs + hidden * gate, 0.0)
                    results.append(result.astype(BF))
                    gradient = gradient * gate * (1.0 + hidden * (1.0 - gate))
                    gradient = jnp.where(live, gradient, 0.0).astype(BF)
                    grad[pair, x] = gradient
                    for a in range(3):
                        at = (x + a) * 2 * LANES + h * LANES
                        shifted[a * channels : (a + 1) * channels, at : at + LANES] = gradient
                store_slots(staging, t, pair, slots, *results)

        convolve_group(matrix, columns, carry_ref, finish)
        total[...] += product(shifted[...], columns[...], ((1,), (1,)))
        return carry

    lax.fori_loop(0, pairs // 2, body, 0)
    height, width = total.shape
    terms[...] = jnp.zeros(terms.shape, F32)
    for tile in range(-(-width // LANES)):
        end = min(width, (tile + 1) * LANES)
        terms[tile * height : (tile + 1) * height, : end - tile * LANES] = total[
            :, tile * LANES : end
        ]
    edge_rows(cells, grad, low_out, high_out, slots, side)
    write_out(staging, out)


def backward_kernel(
    links, counts, field, below_x, above_x, below_y, above_y, upstream, matrix,
    out, table, columns, carry_ref, staging, *, side,
):
    pairs, _, channels, _ = field.shape
    slots = 2 * pairs
    fill_table(table, field, below_x, above_x, below_y, above_y)
    upper = (lane_ids(channels) >= HALF).astype(jnp.int32)

    def body(group, carry):
        build_columns(group, links, table, columns, pairs, side)

        def finish(t, left, right):
            for h in range(2):
                pair = group * 2 + h
                live = 2 * pair + upper < counts[0]
                results = []
                for odd, back in ((0, left), (1, right)):
                    gradient = upstream[pair, 2 * t + odd].astype(F32)
                    gradient = gradient + back[:, h * LANES : (h + 1) * LANES]
                    results.append(jnp.where(live, gradient, 0.0).astype(BF))
                store_slots(staging, t, pair, slots, *results)

        convolve_group(matrix, columns, carry_ref, finish)
        return carry

    lax.fori_loop(0, pairs // 2, body, 0)
    write_out(staging, out)


def unpack_kernel(source, out, *, height, width):
    channels = out.shape[0]
    tiles = -(-width // LANES)
    blocks = []
    for a in range(height // channels):
        for tile in range(tiles):
            start = tile * height + a * channels
            piece = source[start : start + channels, :].astype(F32)
            blocks.append(piece[:, : min(LANES, width - tile * LANES)])
    out[...] = jnp.concatenate(blocks, axis=1)


def call(kernel, out_shape, n_smem, n_vmem, scratch=(), flops=0, moved=4 << 20):
    single = not isinstance(out_shape, (list, tuple))
    return pl.pallas_call(
        kernel,
        out_shape=out_shape,
        in_specs=[SMEM] * n_smem + [VMEM] * n_vmem,
        out_specs=VMEM if single else [VMEM] * len(out_shape),
        scratch_shapes=list(scratch),
        compiler_params=pltpu.CompilerParams(vmem_limit_bytes=56 << 20),
        cost_estimate=pl.CostEstimate(flops=flops, bytes_accessed=moved, transcendentals=0),
    )


def summed(terms, scale):
    axes = ("gx", "gy")
    devices = lax.axis_size("gx") * lax.axis_size("gy")
    me = lax.axis_index("gx") * lax.axis_size("gy") + lax.axis_index("gy")
    bits = [1 << b for b in range(devices.bit_length() - 1)]

    def swapped(block, bit):
        return lax.ppermute(block, axes, [(i, i ^ bit) for i in range(devices)])

    block = terms
    for bit in bits:
        half = block.shape[0] // 2
        mine = me // bit % 2
        kept = lax.dynamic_slice_in_dim(block, mine * half, half, 0)
        sent = lax.dynamic_slice_in_dim(block, (1 - mine) * half, half, 0)
        block = kept + swapped(sent, bit)
    block = (block * scale).astype(BF)
    for bit in bits[::-1]:
        other = swapped(block, bit)
        mine = me // bit % 2
        block = jnp.where(
            mine == 0,
            jnp.concatenate([block, other], axis=0),
            jnp.concatenate([other, block], axis=0),
        )
    return block


def per_device(feats, cotangent, weight, cell_slot, neighbours, counts):
    channels, _, slots, voxels = feats.shape
    side = math.isqrt(cell_slot.shape[1])
    pairs = slots // 2
    cells = cell_slot.reshape(side * side)
    links = neighbours.reshape(slots * 8)
    count = counts.reshape(1)
    native = jax.ShapeDtypeStruct((channels, slots, voxels), BF)
    field = jax.ShapeDtypeStruct((pairs, 8, channels, LANES), BF)
    rows = jax.ShapeDtypeStruct((side // 2, channels, LANES), BF)
    column = jax.ShapeDtypeStruct((4, channels, LANES), BF)
    staging = pltpu.VMEM((4, channels * slots, LANES), F32)
    table = pltpu.VMEM((pairs + 2 + side // 2, 8, channels, LANES), BF)
    columns = pltpu.VMEM((9 * channels, 20 * LANES), BF)
    carry_ref = pltpu.VMEM((channels, 4 * LANES), F32)
    flops = 2 * 27 * channels * channels * slots * voxels

    prepared, low_edge, high_edge = call(
        functools.partial(prepare_kernel, side=side), [field, rows, rows], 1, 1, [staging]
    )(cells, feats.reshape(channels, slots, voxels))
    below_x = passed_along(high_edge, "gx", 1)
    above_x = passed_along(low_edge, "gx", -1)
    upstream = call(regroup_kernel, field, 0, 1, [staging])(
        cotangent.reshape(channels, slots, voxels)
    )
    make_columns = call(functools.partial(column_kernel, side=side), [column, column], 1, 3)
    low_column, high_column = make_columns(cells, prepared, below_x, above_x)
    below_y = from_behind(high_column, "gy", 1)
    above_y = from_behind(low_column, "gy", -1)

    taps = weight.reshape(channels, 3, 9 * channels)
    matrix = taps.transpose(1, 0, 2).reshape(3 * channels, 9 * channels)
    flipped = weight.reshape(channels, 27, channels)[:, ::-1, :].reshape(channels, 3, 9, channels)
    flipped = flipped.transpose(1, 3, 2, 0).reshape(3 * channels, 9 * channels)

    output, grad, terms, low_edge, high_edge = call(
        functools.partial(forward_kernel, side=side),
        [native, field, jax.ShapeDtypeStruct((ROWS, LANES), F32), rows, rows],
        3,
        7,
        [
            table,
            columns,
            pltpu.VMEM((3 * channels, 20 * LANES), BF),
            carry_ref,
            pltpu.VMEM((3 * channels, 9 * channels), F32),
            staging,
        ],
        2 * flops,
    )(cells, links, count, prepared, below_x, above_x, below_y, above_y, upstream, matrix)

    below_x = passed_along(high_edge, "gx", 1)
    above_x = passed_along(low_edge, "gx", -1)
    low_column, high_column = make_columns(cells, grad, below_x, above_x)
    below_y = from_behind(high_column, "gy", 1)
    above_y = from_behind(low_column, "gy", -1)
    grad_feats = call(
        functools.partial(backward_kernel, side=side),
        native,
        2,
        7,
        [table, columns, carry_ref, staging],
        flops,
    )(links, count, grad, below_x, above_x, below_y, above_y, upstream, flipped)

    device_total = lax.axis_size("gx") * lax.axis_size("gy")
    scale = 1.0 / math.sqrt(voxels * slots * device_total)
    grad_weight = call(
        functools.partial(unpack_kernel, height=3 * channels, width=9 * channels),
        jax.ShapeDtypeStruct((channels, 27 * channels), F32),
        0,
        1,
    )(summed(terms, scale))
    return (output.reshape(feats.shape), grad_feats.reshape(feats.shape), grad_weight)


def solution(mesh):
    placed = (
        P(None, "gx", "gy", None),
        P(None, "gx", "gy", None),
        P(),
        P("gx", "gy"),
        P("gx", "gy", None),
        P("gx", "gy"),
    )
    return jax.shard_map(
        per_device,
        mesh=mesh,
        in_specs=placed,
        out_specs=(P(None, "gx", "gy", None), P(None, "gx", "gy", None), P()),
        check_vma=False,
    )
```

```python
import functools
import math

import jax
import jax.numpy as jnp
from jax import lax
from jax.experimental import pallas as pl
from jax.experimental.pallas import tpu as pltpu
from jax.sharding import PartitionSpec as P

BF = jnp.bfloat16
F32 = jnp.float32
VMEM = pl.BlockSpec(memory_space=pltpu.VMEM)
SMEM = pl.BlockSpec(memory_space=pltpu.SMEM)
ANY = pl.BlockSpec(memory_space=pl.ANY)
LANES = 128
HALF = 64
ROWS = 2048


def passed_along(block, axis, distance):
    devices = range(lax.axis_size(axis))
    route = [((i - distance) % len(devices), i) for i in devices]
    return lax.ppermute(block, axis, route)


def from_behind(block, axis, distance):
    devices = range(lax.axis_size(axis))
    route = [(i - distance, i) for i in devices if i - distance in devices]
    return lax.ppermute(block, axis, route)


def lane_ids(channels):
    return lax.broadcasted_iota(jnp.int32, (channels, LANES), 1)


def turn(value, amount):
    return pltpu.roll(value, amount, 1)


def nothing(value):
    return jnp.zeros_like(value)


def load_pairs(source, staging, target):
    channels, slots, _ = source.shape
    low = lane_ids(channels) < HALF
    for tile in range(4):
        piece = source[:, :, tile * LANES : (tile + 1) * LANES].astype(F32)
        staging[tile] = piece.reshape(channels * slots, LANES)

    def body(pair, carry):
        for tile in range(4):
            first = staging[tile, pl.ds(2 * pair, channels, stride=slots), :].astype(BF)
            second = staging[tile, pl.ds(2 * pair + 1, channels, stride=slots), :].astype(BF)
            target[pair, 2 * tile] = jnp.where(low, first, turn(second, HALF))
            target[pair, 2 * tile + 1] = jnp.where(low, turn(first, HALF), second)
        return carry

    lax.fori_loop(0, slots // 2, body, 0)


def edge_rows(cells, field, low_out, high_out, slots, side):
    channels = field.shape[2]
    low = lane_ids(channels) < HALF
    for out, line, layer in ((low_out, 0, 0), (high_out, side - 1, 7)):
        for tile in range(side // 2):
            parts = []
            for part in range(2):
                slot = cells[line * side + 2 * tile + part]
                row = field[jnp.minimum(slot, slots - 1) // 2, layer]
                row = turn(row, (part + slot) % 2 * HALF)
                parts.append(jnp.where(slot < slots, row, nothing(row)))
            out[tile] = jnp.where(low, parts[0], parts[1])


def prepare_kernel(cells, feats, pairs, low_out, high_out, staging, *, side):
    load_pairs(feats, staging, pairs)
    edge_rows(cells, pairs, low_out, high_out, feats.shape[1], side)


def regroup_kernel(source, pairs, staging):
    load_pairs(source, staging, pairs)


def column_kernel(cells, field, below, above, low_out, high_out, *, side):
    channels = field.shape[2]
    slots = 2 * field.shape[0]
    lanes = lane_ids(channels)
    for out, line, place in ((low_out, 0, 0), (high_out, side - 1, 56)):
        corner = line % 2 * HALF + place
        for quarter in range(4):
            total = jnp.zeros((channels, LANES), BF)
            for half in range(2):
                layer = quarter + 4 * half
                for u in range(1, side + 1):
                    slot = cells[(u - 1) * side + line]
                    row = field[jnp.minimum(slot, slots - 1) // 2, layer]
                    goal = half * HALF + u * 8
                    row = turn(row, (goal - place + LANES - slot % 2 * HALF) % LANES)
                    row = jnp.where(slot < slots, row, nothing(row))
                    total = jnp.where(lanes // 8 == goal // 8, row, total)
                if layer == 7:
                    goal = half * HALF
                    row = turn(below[line // 2], (goal - corner) % LANES)
                    total = jnp.where(lanes // 8 == goal // 8, row, total)
                if layer == 0:
                    goal = half * HALF + (side + 1) * 8
                    row = turn(above[line // 2], (goal - corner) % LANES)
                    total = jnp.where(lanes // 8 == goal // 8, row, total)
            out[quarter] = total


def fill_table(table, field, below_x, above_x, below_y, above_y, sem):
    pairs, _, channels, _ = field.shape
    low = lane_ids(channels) < HALF
    copy = pltpu.make_async_copy(field, table.at[pl.ds(0, pairs)], sem)
    copy.start()
    for quarter in range(4):
        below, above = below_y[quarter], above_y[quarter]
        table[pairs, quarter] = jnp.where(low, below, turn(above, HALF))
        table[pairs, quarter + 4] = jnp.where(low, turn(below, HALF), above)
    tiles = below_x.shape[0]
    for tile in range(tiles):
        table[pairs + 1 + tile, 7] = below_x[tile]
        table[pairs + 1 + tile, 0] = above_x[tile]
    table[pairs + 1 + tiles] = jnp.zeros(table.shape[1:], BF)
    copy.wait()


def locate(index, pairs, side, column):
    slots = 2 * pairs
    tiles = side // 2
    wide = side + 2
    place = 0 if column is None else column * 8
    own = index < slots
    row = index < slots + 2 * side
    below = index < slots + side
    ordinal = jnp.where(own, index, index - slots - jnp.where(below, 0, side))
    base = jnp.where(own, 0, pairs + 1)
    tile_row = base + ordinal // 2
    lane_row = ordinal % 2 * HALF + place
    last = index >= slots + 2 * side + 2 * wide
    u = index - slots - 2 * side
    lane_column = jnp.where(u < wide, u * 8, HALF + (u - wide) * 8)
    tile = jnp.where(row, tile_row, jnp.where(last, pairs + 1 + tiles, pairs))
    lane = jnp.where(row, lane_row, jnp.where(last, 0, lane_column))
    return tile, lane


def column_builder(group, links, table, columns, pairs, side):
    channels = table.shape[2]
    lanes = lane_ids(channels)
    low = lanes < HALF
    y_first = lanes % HALF < 8
    y_last = lanes % HALF >= 56
    z_first = lanes % 8 == 0
    z_last = lanes % 8 == 7
    spots = {}
    for h in range(2):
        for part in range(2):
            slot = group * 4 + 2 * h + part
            for k, (dx, dy) in enumerate(
                ((-1, -1), (-1, 0), (-1, 1), (0, -1), (0, 1), (1, -1), (1, 0), (1, 1))
            ):
                column = {-1: 7, 0: None, 1: 0}[dy]
                goal = part * HALF + (56 if dy == 1 else 0)
                tile, lane = locate(links[slot * 8 + k], pairs, side, column)
                spots[h, part, dx, dy] = tile, (goal + LANES - lane) % LANES

    def fetch(layer, h, dx, dy):
        rows = []
        for part in range(2):
            tile, amount = spots[h, part, dx, dy]
            rows.append(turn(table[tile, layer], amount))
        return jnp.where(low, rows[0], rows[1])

    def layer_of(xp, layer, dx):
        for h in range(2):
            if dx == 0:
                middle = table[group * 2 + h, layer]
            else:
                middle = fetch(layer, h, dx, 0)
            before = jnp.where(y_first, fetch(layer, h, dx, -1), turn(middle, 8))
            after = jnp.where(y_last, fetch(layer, h, dx, 1), turn(middle, LANES - 8))
            at = xp * 2 * LANES + h * LANES
            for b, value in enumerate((before, middle, after)):
                lower = jnp.where(z_first, nothing(value), turn(value, 1))
                upper = jnp.where(z_last, nothing(value), turn(value, LANES - 1))
                for c, shifted in enumerate((lower, value, upper)):
                    start = (b * 3 + c) * channels
                    columns[start : start + channels, at : at + LANES] = shifted

    def build(xp):
        if xp == 0:
            layer_of(0, 7, -1)
        elif xp == 9:
            layer_of(9, 0, 1)
        else:
            layer_of(xp, xp - 1, 0)

    return build


def product(left, right, contract):
    return lax.dot_general(left, right, (contract, ((), ())), preferred_element_type=F32)


def convolve_group(matrix, columns, carry_ref, build, finish):
    channels = matrix.shape[0] // 3
    width = 2 * LANES
    build(0)
    build(1)
    for step in range(5):
        if step < 4:
            build(2 * step + 2)
            build(2 * step + 3)
        part = product(
            matrix[...], columns[:, step * 2 * width : (step + 1) * 2 * width], ((1,), (0,))
        )
        first, second, third = (part[a * channels : (a + 1) * channels] for a in range(3))
        if step > 0:
            left = carry_ref[:, :width] + third[:, :width]
            right = carry_ref[:, width:] + (second[:, :width] + third[:, width:])
            finish(step - 1, left, right)
        if step < 4:
            carry_ref[:, :width] = first[:, :width] + second[:, width:]
            carry_ref[:, width:] = first[:, width:]


def store_slots(staging, t, pair, slots, even, odd):
    channels = even.shape[0]
    low = lane_ids(channels) < HALF
    first = jnp.where(low, even, turn(odd, HALF))
    second = jnp.where(low, turn(even, HALF), odd)
    staging[t, pl.ds(2 * pair, channels, stride=slots), :] = first.astype(F32)
    staging[t, pl.ds(2 * pair + 1, channels, stride=slots), :] = second.astype(F32)


def write_out(staging, out):
    channels, slots, _ = out.shape
    for tile in range(4):
        out[:, :, tile * LANES : (tile + 1) * LANES] = (
            staging[tile].reshape(channels, slots, LANES).astype(BF)
        )


def forward_kernel(
    cells, links, counts, below_x, above_x, below_y, above_y, matrix, field, given,
    out, grad, terms, low_out, high_out,
    table, columns, shifted, carry_ref, total, upstream, sems, *, side,
):
    pairs, _, channels, _ = field.shape
    slots = 2 * pairs
    copy = pltpu.make_async_copy(given, upstream, sems.at[1])
    copy.start()
    fill_table(table, field, below_x, above_x, below_y, above_y, sems.at[0])
    total[...] = jnp.zeros(total.shape, F32)
    shifted[...] = jnp.zeros(shifted.shape, BF)
    upper = (lane_ids(channels) >= HALF).astype(jnp.int32)
    copy.wait()

    def body(group, carry):
        build = column_builder(group, links, table, columns, pairs, side)

        def finish(t, left, right):
            for h in range(2):
                pair = group * 2 + h
                live = 2 * pair + upper < counts[0]
                for odd, hidden in ((0, left), (1, right)):
                    x = 2 * t + odd
                    hidden = hidden[:, h * LANES : (h + 1) * LANES]
                    gate = jax.nn.sigmoid(hidden)
                    inputs = table[pair, x].astype(F32)
                    gradient = upstream[pair, x].astype(F32)
                    result = jnp.where(live, inputs + hidden * gate, 0.0)
                    out[pair, x] = result.astype(BF)
                    gradient = gradient * gate * (1.0 + hidden * (1.0 - gate))
                    gradient = jnp.where(live, gradient, 0.0).astype(BF)
                    grad[pair, x] = gradient
                    for a in range(3):
                        at = (x + a) * 2 * LANES + h * LANES
                        shifted[a * channels : (a + 1) * channels, at : at + LANES] = gradient
            gather_terms(t)

        def gather_terms(step):
            span = slice(step * 4 * LANES, (step + 1) * 4 * LANES)
            total[...] += product(shifted[:, span], columns[:, span], ((1,), (1,)))

        convolve_group(matrix, columns, carry_ref, build, finish)
        gather_terms(4)
        return carry

    lax.fori_loop(0, pairs // 2, body, 0)
    height, width = total.shape
    terms[...] = jnp.zeros(terms.shape, F32)
    for tile in range(-(-width // LANES)):
        end = min(width, (tile + 1) * LANES)
        terms[tile * height : (tile + 1) * height, : end - tile * LANES] = total[
            :, tile * LANES : end
        ]
    edge_rows(cells, grad, low_out, high_out, slots, side)


def backward_kernel(
    links, counts, below_x, above_x, below_y, above_y, matrix, field, given,
    out, table, columns, carry_ref, upstream, sems, *, side, group,
):
    pairs, _, channels, _ = field.shape
    copy = pltpu.make_async_copy(given.at[pl.ds(2 * group, 2)], upstream, sems.at[1])
    copy.start()
    fill_table(table, field, below_x, above_x, below_y, above_y, sems.at[0])
    upper = (lane_ids(channels) >= HALF).astype(jnp.int32)
    build = column_builder(group, links, table, columns, pairs, side)

    def finish(t, left, right):
        for h in range(2):
            live = 2 * (group * 2 + h) + upper < counts[0]
            for odd, back in ((0, left), (1, right)):
                x = 2 * t + odd
                gradient = upstream[h, x].astype(F32) + back[:, h * LANES : (h + 1) * LANES]
                out[h, x] = jnp.where(live, gradient, 0.0).astype(BF)

    copy.wait()
    convolve_group(matrix, columns, carry_ref, build, finish)


def native_kernel(*refs):
    *parts, out, staging = refs
    slots = out.shape[1]
    count = parts[0].shape[0]
    for index, part in enumerate(parts):

        def body(pair, carry, index=index, part=part):
            for t in range(4):
                even, odd = part[pair, 2 * t], part[pair, 2 * t + 1]
                store_slots(staging, t, index * count + pair, slots, even, odd)
            return carry

        lax.fori_loop(0, count, body, 0)
    write_out(staging, out)


def unpack_kernel(source, out, *, height, width):
    channels = out.shape[0]
    tiles = -(-width // LANES)
    blocks = []
    for a in range(height // channels):
        for tile in range(tiles):
            start = tile * height + a * channels
            piece = source[start : start + channels, :].astype(F32)
            blocks.append(piece[:, : min(LANES, width - tile * LANES)])
    out[...] = jnp.concatenate(blocks, axis=1)


def call(kernel, out_shape, n_smem, n_vmem, scratch=(), flops=0, moved=4 << 20, n_any=0):
    single = not isinstance(out_shape, (list, tuple))
    return pl.pallas_call(
        kernel,
        out_shape=out_shape,
        in_specs=[SMEM] * n_smem + [VMEM] * n_vmem + [ANY] * n_any,
        out_specs=VMEM if single else [VMEM] * len(out_shape),
        scratch_shapes=list(scratch),
        compiler_params=pltpu.CompilerParams(vmem_limit_bytes=56 << 20),
        cost_estimate=pl.CostEstimate(flops=flops, bytes_accessed=moved, transcendentals=0),
    )


def tied(value, *others):
    return lax.optimization_barrier((value, *others))[0]


def summed(terms, scale, tasks):
    axes = ("gx", "gy")
    devices = lax.axis_size("gx") * lax.axis_size("gy")
    me = lax.axis_index("gx") * lax.axis_size("gy") + lax.axis_index("gy")
    bits = [1 << b for b in range(devices.bit_length() - 1)]

    def swapped(block, bit):
        return lax.ppermute(block, axes, [(i, i ^ bit) for i in range(devices)])

    block = terms
    for step, bit in enumerate(bits + bits[::-1]):
        beside = tasks[step](block) if step in tasks else None
        mine = me // bit % 2
        if step < len(bits):
            half = block.shape[0] // 2
            kept = lax.dynamic_slice_in_dim(block, mine * half, half, 0)
            sent = lax.dynamic_slice_in_dim(block, (1 - mine) * half, half, 0)
            block = kept + swapped(sent, bit)
            if step == len(bits) - 1:
                block = (block * scale).astype(BF)
        else:
            other = swapped(block, bit)
            block = jnp.where(
                mine == 0,
                jnp.concatenate([block, other], axis=0),
                jnp.concatenate([other, block], axis=0),
            )
        if beside is not None:
            block = tied(block, beside)
    return block


def per_device(feats, cotangent, weight, cell_slot, neighbours, counts):
    channels, _, slots, voxels = feats.shape
    side = math.isqrt(cell_slot.shape[1])
    pairs = slots // 2
    cells = cell_slot.reshape(side * side)
    links = neighbours.reshape(slots * 8)
    count = counts.reshape(1)
    native = jax.ShapeDtypeStruct((channels, slots, voxels), BF)
    field = jax.ShapeDtypeStruct((pairs, 8, channels, LANES), BF)
    rows = jax.ShapeDtypeStruct((side // 2, channels, LANES), BF)
    column = jax.ShapeDtypeStruct((4, channels, LANES), BF)
    staging = pltpu.VMEM((4, channels * slots, LANES), F32)
    table = pltpu.VMEM((pairs + 2 + side // 2, 8, channels, LANES), BF)
    columns = pltpu.VMEM((9 * channels, 20 * LANES), BF)
    carry_ref = pltpu.VMEM((channels, 4 * LANES), F32)
    sems = pltpu.SemaphoreType.DMA((2,))
    flops = 2 * 27 * channels * channels * slots * voxels

    prepared, low_edge, high_edge = call(
        functools.partial(prepare_kernel, side=side), [field, rows, rows], 1, 1, [staging]
    )(cells, feats.reshape(channels, slots, voxels))
    below_x = passed_along(high_edge, "gx", 1)
    above_x = passed_along(low_edge, "gx", -1)
    upstream = call(regroup_kernel, field, 0, 1, [staging])(
        cotangent.reshape(channels, slots, voxels)
    )
    make_columns = call(functools.partial(column_kernel, side=side), [column, column], 1, 3)
    low_column, high_column = make_columns(cells, tied(prepared, upstream), below_x, above_x)
    below_y = from_behind(high_column, "gy", 1)
    above_y = from_behind(low_column, "gy", -1)

    taps = weight.reshape(channels, 3, 9 * channels)
    matrix = taps.transpose(1, 0, 2).reshape(3 * channels, 9 * channels)
    flipped = weight.reshape(channels, 27, channels)[:, ::-1, :].reshape(channels, 3, 9, channels)
    flipped = flipped.transpose(1, 3, 2, 0).reshape(3 * channels, 9 * channels)

    output, grad, terms, low_edge, high_edge = call(
        functools.partial(forward_kernel, side=side),
        [field, field, jax.ShapeDtypeStruct((ROWS, LANES), F32), rows, rows],
        3,
        5,
        [
            table,
            columns,
            pltpu.VMEM((3 * channels, 20 * LANES), BF),
            carry_ref,
            pltpu.VMEM((3 * channels, 9 * channels), F32),
            pltpu.VMEM(field.shape, BF),
            sems,
        ],
        2 * flops,
        n_any=2,
    )(cells, links, count, below_x, above_x, below_y, above_y, matrix, prepared, upstream)

    halos = [passed_along(high_edge, "gx", 1), passed_along(low_edge, "gx", -1)]
    parts = []
    done = {}

    def columns_task(token):
        low_column, high_column = make_columns(cells, tied(grad, token), *halos)
        halos.append(from_behind(high_column, "gy", 1))
        halos.append(from_behind(low_column, "gy", -1))
        return low_column

    def output_task(token):
        done["output"] = call(native_kernel, native, 0, 1, [staging])(tied(output, token))
        return done["output"]

    def backward_task(group, token):
        part = call(
            functools.partial(backward_kernel, side=side, group=group),
            jax.ShapeDtypeStruct((2, 8, channels, LANES), BF),
            2,
            5,
            [table, columns, carry_ref, pltpu.VMEM((2, 8, channels, LANES), BF), sems],
            4 * flops // pairs,
            n_any=2,
        )(links, count, *halos, flipped, tied(grad, token), upstream)
        parts.append(part)
        return part

    def gradient_task(token):
        first = tied(parts[0], token)
        done["grad"] = call(native_kernel, native, 0, len(parts), [staging])(first, *parts[1:])
        return done["grad"]

    tasks = [columns_task, output_task]
    tasks += [functools.partial(backward_task, group) for group in range(pairs // 2)]
    tasks += [gradient_task]
    device_total = lax.axis_size("gx") * lax.axis_size("gy")
    scale = 1.0 / math.sqrt(voxels * slots * device_total)
    whole = summed(terms, scale, dict(enumerate(tasks, 1)))
    grad_weight = call(
        functools.partial(unpack_kernel, height=3 * channels, width=9 * channels),
        jax.ShapeDtypeStruct((channels, 27 * channels), F32),
        0,
        1,
    )(whole)
    return (done["output"].reshape(feats.shape), done["grad"].reshape(feats.shape), grad_weight)


def solution(mesh):
    placed = (
        P(None, "gx", "gy", None),
        P(None, "gx", "gy", None),
        P(),
        P("gx", "gy"),
        P("gx", "gy", None),
        P("gx", "gy"),
    )
    return jax.shard_map(
        per_device,
        mesh=mesh,
        in_specs=placed,
        out_specs=(P(None, "gx", "gy", None), P(None, "gx", "gy", None), P()),
        check_vma=False,
    )
```

```python
import functools
import math

import jax
import jax.numpy as jnp
from jax import lax
from jax.experimental import pallas as pl
from jax.experimental.pallas import tpu as pltpu
from jax.sharding import PartitionSpec as P

BF = jnp.bfloat16
F32 = jnp.float32
VMEM = pl.BlockSpec(memory_space=pltpu.VMEM)
SMEM = pl.BlockSpec(memory_space=pltpu.SMEM)
ANY = pl.BlockSpec(memory_space=pl.ANY)
LANES = 128
HALF = 64
ROWS = 2048


def passed_along(block, axis, distance):
    devices = range(lax.axis_size(axis))
    route = [((i - distance) % len(devices), i) for i in devices]
    return lax.ppermute(block, axis, route)


def from_behind(block, axis, distance):
    devices = range(lax.axis_size(axis))
    route = [(i - distance, i) for i in devices if i - distance in devices]
    return lax.ppermute(block, axis, route)


def lane_ids(channels):
    return lax.broadcasted_iota(jnp.int32, (channels, LANES), 1)


def turn(value, amount):
    return pltpu.roll(value, amount, 1)


def nothing(value):
    return jnp.zeros_like(value)


def load_pairs(source, target):
    channels, slots, _ = source.shape
    low = lane_ids(channels) < HALF
    for tile in range(4):
        rows = jnp.swapaxes(source[:, :, tile * LANES : (tile + 1) * LANES], 0, 1)
        for pair in range(slots // 2):
            first, second = rows[2 * pair], rows[2 * pair + 1]
            target[pair, 2 * tile] = jnp.where(low, first, turn(second, HALF))
            target[pair, 2 * tile + 1] = jnp.where(low, turn(first, HALF), second)


def edge_rows(cells, field, low_out, high_out, slots, side):
    channels = field.shape[2]
    low = lane_ids(channels) < HALF
    for out, line, layer in ((low_out, 0, 0), (high_out, side - 1, 7)):
        for tile in range(side // 2):
            parts = []
            for part in range(2):
                slot = cells[line * side + 2 * tile + part]
                row = field[jnp.minimum(slot, slots - 1) // 2, layer]
                row = turn(row, (part + slot) % 2 * HALF)
                parts.append(jnp.where(slot < slots, row, nothing(row)))
            out[tile] = jnp.where(low, parts[0], parts[1])


def prepare_kernel(cells, feats, pairs, low_out, high_out, *, side):
    load_pairs(feats, pairs)
    edge_rows(cells, pairs, low_out, high_out, feats.shape[1], side)


def regroup_kernel(source, pairs):
    load_pairs(source, pairs)


def weights_kernel(weight, matrix, flipped):
    channels = weight.shape[0]
    width = 9 * channels
    for a in range(3):
        rows = slice(a * channels, (a + 1) * channels)
        matrix[rows, :] = weight[:, a * width : (a + 1) * width]
        blocks = []
        for bc in range(9):
            tap = 26 - (a * 9 + bc)
            blocks.append(weight[:, tap * channels : (tap + 1) * channels].T)
        flipped[rows, :] = jnp.concatenate(blocks, axis=1)


def column_kernel(cells, field, below, above, low_out, high_out, *, side):
    channels = field.shape[2]
    slots = 2 * field.shape[0]
    lanes = lane_ids(channels)
    for out, line, place in ((low_out, 0, 0), (high_out, side - 1, 56)):
        corner = line % 2 * HALF + place
        for quarter in range(4):
            total = jnp.zeros((channels, LANES), BF)
            for half in range(2):
                layer = quarter + 4 * half
                for u in range(1, side + 1):
                    slot = cells[(u - 1) * side + line]
                    row = field[jnp.minimum(slot, slots - 1) // 2, layer]
                    goal = half * HALF + u * 8
                    row = turn(row, (goal - place + LANES - slot % 2 * HALF) % LANES)
                    row = jnp.where(slot < slots, row, nothing(row))
                    total = jnp.where(lanes // 8 == goal // 8, row, total)
                if layer == 7:
                    goal = half * HALF
                    row = turn(below[line // 2], (goal - corner) % LANES)
                    total = jnp.where(lanes // 8 == goal // 8, row, total)
                if layer == 0:
                    goal = half * HALF + (side + 1) * 8
                    row = turn(above[line // 2], (goal - corner) % LANES)
                    total = jnp.where(lanes // 8 == goal // 8, row, total)
            out[quarter] = total


def fill_table(table, field, below_x, above_x, below_y, above_y, sem):
    pairs, _, channels, _ = field.shape
    low = lane_ids(channels) < HALF
    copy = pltpu.make_async_copy(field, table.at[pl.ds(0, pairs)], sem)
    copy.start()
    for quarter in range(4):
        below, above = below_y[quarter], above_y[quarter]
        table[pairs, quarter] = jnp.where(low, below, turn(above, HALF))
        table[pairs, quarter + 4] = jnp.where(low, turn(below, HALF), above)
    tiles = below_x.shape[0]
    for tile in range(tiles):
        table[pairs + 1 + tile, 7] = below_x[tile]
        table[pairs + 1 + tile, 0] = above_x[tile]
    table[pairs + 1 + tiles] = jnp.zeros(table.shape[1:], BF)
    copy.wait()


def locate(index, pairs, side, column):
    slots = 2 * pairs
    tiles = side // 2
    wide = side + 2
    place = 0 if column is None else column * 8
    own = index < slots
    row = index < slots + 2 * side
    below = index < slots + side
    ordinal = jnp.where(own, index, index - slots - jnp.where(below, 0, side))
    base = jnp.where(own, 0, pairs + 1)
    tile_row = base + ordinal // 2
    lane_row = ordinal % 2 * HALF + place
    last = index >= slots + 2 * side + 2 * wide
    u = index - slots - 2 * side
    lane_column = jnp.where(u < wide, u * 8, HALF + (u - wide) * 8)
    tile = jnp.where(row, tile_row, jnp.where(last, pairs + 1 + tiles, pairs))
    lane = jnp.where(row, lane_row, jnp.where(last, 0, lane_column))
    return tile, lane


def column_builder(group, links, table, columns, pairs, side):
    channels = table.shape[2]
    lanes = lane_ids(channels)
    low = lanes < HALF
    y_first = lanes % HALF < 8
    y_last = lanes % HALF >= 56
    z_first = lanes % 8 == 0
    z_last = lanes % 8 == 7
    spots = {}
    for h in range(2):
        for part in range(2):
            slot = group * 4 + 2 * h + part
            for k, (dx, dy) in enumerate(
                ((-1, -1), (-1, 0), (-1, 1), (0, -1), (0, 1), (1, -1), (1, 0), (1, 1))
            ):
                column = {-1: 7, 0: None, 1: 0}[dy]
                goal = part * HALF + (56 if dy == 1 else 0)
                tile, lane = locate(links[k, slot], pairs, side, column)
                spots[h, part, dx, dy] = tile, (goal + LANES - lane) % LANES

    def fetch(layer, h, dx, dy):
        rows = []
        for part in range(2):
            tile, amount = spots[h, part, dx, dy]
            rows.append(turn(table[tile, layer], amount))
        return jnp.where(low, rows[0], rows[1])

    def layer_of(xp, layer, dx):
        for h in range(2):
            if dx == 0:
                middle = table[group * 2 + h, layer]
            else:
                middle = fetch(layer, h, dx, 0)
            before = jnp.where(y_first, fetch(layer, h, dx, -1), turn(middle, 8))
            after = jnp.where(y_last, fetch(layer, h, dx, 1), turn(middle, LANES - 8))
            at = xp * 2 * LANES + h * LANES
            for b, value in enumerate((before, middle, after)):
                lower = jnp.where(z_first, nothing(value), turn(value, 1))
                upper = jnp.where(z_last, nothing(value), turn(value, LANES - 1))
                for c, shifted in enumerate((lower, value, upper)):
                    start = (b * 3 + c) * channels
                    columns[start : start + channels, at : at + LANES] = shifted

    def build(xp):
        if xp == 0:
            layer_of(0, 7, -1)
        elif xp == 9:
            layer_of(9, 0, 1)
        else:
            layer_of(xp, xp - 1, 0)

    return build


def product(left, right, contract):
    return lax.dot_general(left, right, (contract, ((), ())), preferred_element_type=F32)


def convolve_group(matrix, columns, carry_ref, build, finish):
    channels = matrix.shape[0] // 3
    width = 2 * LANES
    build(0)
    build(1)
    for step in range(5):
        if step < 4:
            build(2 * step + 2)
            build(2 * step + 3)
        part = product(
            matrix[...], columns[:, step * 2 * width : (step + 1) * 2 * width], ((1,), (0,))
        )
        first, second, third = (part[a * channels : (a + 1) * channels] for a in range(3))
        if step > 0:
            left = carry_ref[:, :width] + third[:, :width]
            right = carry_ref[:, width:] + (second[:, :width] + third[:, width:])
            finish(step - 1, left, right)
        if step < 4:
            carry_ref[:, :width] = first[:, :width] + second[:, width:]
            carry_ref[:, width:] = first[:, width:]


def forward_kernel(
    cells, links, counts, mine, below_x, above_x, below_y, above_y, matrix, field, given,
    out, grad, kept, sent, low_out, high_out,
    table, columns, shifted, carry_ref, total, terms, upstream, sems, *, side,
):
    pairs, _, channels, _ = field.shape
    slots = 2 * pairs
    copy = pltpu.make_async_copy(given, upstream, sems.at[1])
    copy.start()
    fill_table(table, field, below_x, above_x, below_y, above_y, sems.at[0])
    total[...] = jnp.zeros(total.shape, F32)
    shifted[...] = jnp.zeros(shifted.shape, BF)
    upper = (lane_ids(channels) >= HALF).astype(jnp.int32)
    copy.wait()

    def body(group, carry):
        build = column_builder(group, links, table, columns, pairs, side)

        def finish(t, left, right):
            for h in range(2):
                pair = group * 2 + h
                live = 2 * pair + upper < counts[0]
                for odd, hidden in ((0, left), (1, right)):
                    x = 2 * t + odd
                    hidden = hidden[:, h * LANES : (h + 1) * LANES]
                    gate = jax.nn.sigmoid(hidden)
                    inputs = table[pair, x].astype(F32)
                    gradient = upstream[pair, x].astype(F32)
                    result = jnp.where(live, inputs + hidden * gate, 0.0)
                    out[pair, x] = result.astype(BF)
                    gradient = gradient * gate * (1.0 + hidden * (1.0 - gate))
                    gradient = jnp.where(live, gradient, 0.0).astype(BF)
                    grad[pair, x] = gradient
                    for a in range(3):
                        at = (x + a) * 2 * LANES + h * LANES
                        shifted[a * channels : (a + 1) * channels, at : at + LANES] = gradient
            gather_terms(t)

        def gather_terms(step):
            span = slice(step * 4 * LANES, (step + 1) * 4 * LANES)
            total[...] += product(shifted[:, span], columns[:, span], ((1,), (1,)))

        convolve_group(matrix, columns, carry_ref, build, finish)
        gather_terms(4)
        return carry

    lax.fori_loop(0, pairs // 2, body, 0)
    height, width = total.shape
    terms[...] = jnp.zeros(terms.shape, F32)
    for tile in range(-(-width // LANES)):
        end = min(width, (tile + 1) * LANES)
        terms[tile * height : (tile + 1) * height, : end - tile * LANES] = total[
            :, tile * LANES : end
        ]
    half = kept.shape[0]
    kept[...] = terms[pl.ds(pl.multiple_of(mine[0] * half, half), half), :]
    sent[...] = terms[pl.ds(pl.multiple_of((1 - mine[0]) * half, half), half), :]
    edge_rows(cells, grad, low_out, high_out, slots, side)


def backward_kernel(
    links, counts, below_x, above_x, below_y, above_y, matrix, field, given,
    out, table, columns, carry_ref, upstream, sems, *, side, group,
):
    pairs, _, channels, _ = field.shape
    copy = pltpu.make_async_copy(given.at[pl.ds(2 * group, 2)], upstream, sems.at[1])
    copy.start()
    fill_table(table, field, below_x, above_x, below_y, above_y, sems.at[0])
    upper = (lane_ids(channels) >= HALF).astype(jnp.int32)
    build = column_builder(group, links, table, columns, pairs, side)

    def finish(t, left, right):
        for h in range(2):
            live = 2 * (group * 2 + h) + upper < counts[0]
            for odd, back in ((0, left), (1, right)):
                x = 2 * t + odd
                gradient = upstream[h, x].astype(F32) + back[:, h * LANES : (h + 1) * LANES]
                out[h, x] = jnp.where(live, gradient, 0.0).astype(BF)

    copy.wait()
    convolve_group(matrix, columns, carry_ref, build, finish)


def native_kernel(*refs):
    *parts, out = refs
    low = lane_ids(out.shape[0]) < HALF
    for t in range(4):
        rows = []
        for part in parts:
            for pair in range(part.shape[0]):
                even, odd = part[pair, 2 * t], part[pair, 2 * t + 1]
                rows.append(jnp.where(low, even, turn(odd, HALF)))
                rows.append(jnp.where(low, turn(even, HALF), odd))
        out[:, :, t * LANES : (t + 1) * LANES] = jnp.swapaxes(jnp.stack(rows), 0, 1)


def unpack_kernel(mine, block, received, out, joined, *, height, width):
    join_kernel(mine, block, received, joined)
    channels = out.shape[0]
    tiles = -(-width // LANES)
    blocks = []
    for a in range(height // channels):
        for tile in range(tiles):
            start = tile * height + a * channels
            piece = joined[start : start + channels, :].astype(F32)
            blocks.append(piece[:, : min(LANES, width - tile * LANES)])
    out[...] = jnp.concatenate(blocks, axis=1)


def call(kernel, out_shape, n_smem, n_vmem, scratch=(), flops=0, n_any=0, room=10, after=()):
    inputs, outputs = n_smem + n_vmem + n_any, len(out_shape)

    def body(*refs):
        refs, marks = refs[:inputs], refs[inputs + len(after) :]
        kernel(*refs, *marks[:outputs], *marks[outputs + 1 :])
        marks[outputs][...] = jnp.zeros((8, LANES), F32)

    called = pl.pallas_call(
        body,
        out_shape=[*out_shape, jax.ShapeDtypeStruct((8, LANES), F32)],
        in_specs=[SMEM] * n_smem + [VMEM] * n_vmem + [ANY] * (n_any + len(after)),
        out_specs=[VMEM] * (outputs + 1),
        scratch_shapes=list(scratch),
        compiler_params=pltpu.CompilerParams(vmem_limit_bytes=room << 20),
        cost_estimate=pl.CostEstimate(flops=flops, bytes_accessed=4 << 20, transcendentals=0),
    )
    return lambda *args: called(*args, *after)


def split_kernel(mine, kept, received, kept_out, sent_out):
    half = kept_out.shape[0]
    here = pl.multiple_of(mine[0] * half, half)
    there = pl.multiple_of((1 - mine[0]) * half, half)
    kept_out[...] = kept[pl.ds(here, half), :] + received[pl.ds(here, half), :]
    sent_out[...] = kept[pl.ds(there, half), :] + received[pl.ds(there, half), :]


def add_kernel(kept, received, out, *, scale):
    total = kept[...] + received[...]
    out[...] = total if scale is None else (total * scale).astype(BF)


def join_kernel(mine, block, received, out):
    half = block.shape[0]
    out[pl.ds(pl.multiple_of(mine[0] * half, half), half), :] = block[...]
    out[pl.ds(pl.multiple_of((1 - mine[0]) * half, half), half), :] = received[...]


def sum_bits():
    devices = lax.axis_size("gx") * lax.axis_size("gy")
    bits = [1 << b for b in range(devices.bit_length() - 1)]
    inner = [bit for bit in bits if bit < lax.axis_size("gy")]
    return inner, bits[len(inner) :]


def bit_of_me(bit):
    me = lax.axis_index("gx") * lax.axis_size("gy") + lax.axis_index("gy")
    return (me // bit % 2).reshape(1)


def summed(kept, sent, mark, scale, tasks):
    axes = ("gx", "gy")
    devices = lax.axis_size("gx") * lax.axis_size("gy")
    inner, outer = sum_bits()

    def swapped(block, bit):
        return lax.ppermute(block, axes, [(i, i ^ bit) for i in range(devices)])

    def like(block, factor, kind=F32):
        return jax.ShapeDtypeStruct((int(block.shape[0] * factor), LANES), kind)

    order = inner + outer + inner[::-1]
    block = kept
    for step, bit in enumerate(order):
        received = swapped(sent if step < len(inner) else block, bit)
        after = [tasks[step](mark)] if step in tasks else []
        if step + 1 < len(inner):
            half = like(block, 0.5)
            block, sent, mark = call(split_kernel, [half, half], 1, 2, after=after)(
                bit_of_me(order[step + 1]), block, received
            )
        elif step < len(inner) + len(outer):
            last = step + 1 == len(inner) + len(outer)
            kernel = functools.partial(add_kernel, scale=scale if last else None)
            block, mark = call(kernel, [like(block, 1, BF if last else F32)], 0, 2, after=after)(
                block, received
            )
        elif step + 1 < len(order):
            block, mark = call(join_kernel, [like(block, 2, BF)], 1, 2, after=after)(
                bit_of_me(bit), block, received
            )
        else:
            return bit_of_me(bit), block, received, after


def per_device(feats, cotangent, weight, cell_slot, neighbours, counts):
    channels, _, slots, voxels = feats.shape
    side = math.isqrt(cell_slot.shape[1])
    pairs = slots // 2
    cells = cell_slot.reshape(side * side)
    links = neighbours.reshape(slots, 8).T
    count = counts.reshape(1)
    native = jax.ShapeDtypeStruct((channels, slots, voxels), BF)
    field = jax.ShapeDtypeStruct((pairs, 8, channels, LANES), BF)
    rows = jax.ShapeDtypeStruct((side // 2, channels, LANES), BF)
    column = jax.ShapeDtypeStruct((4, channels, LANES), BF)
    table = pltpu.VMEM((pairs + 2 + side // 2, 8, channels, LANES), BF)
    columns = pltpu.VMEM((9 * channels, 20 * LANES), BF)
    carry_ref = pltpu.VMEM((channels, 4 * LANES), F32)
    sems = pltpu.SemaphoreType.DMA((2,))
    flops = 2 * 27 * channels * channels * slots * voxels

    prepared, low_edge, high_edge, _ = call(
        functools.partial(prepare_kernel, side=side), [field, rows, rows], 1, 1
    )(cells, feats.reshape(channels, slots, voxels))
    below_x = passed_along(high_edge, "gx", 1)
    above_x = passed_along(low_edge, "gx", -1)
    upstream, mark = call(regroup_kernel, [field], 0, 1)(
        cotangent.reshape(channels, slots, voxels)
    )
    make_columns = functools.partial(column_kernel, side=side)
    low_column, high_column, mark = call(make_columns, [column, column], 1, 3, after=[mark])(
        cells, prepared, below_x, above_x
    )
    below_y = from_behind(high_column, "gy", 1)
    above_y = from_behind(low_column, "gy", -1)
    stacked = jax.ShapeDtypeStruct((3 * channels, 9 * channels), BF)
    matrix, flipped, _ = call(weights_kernel, [stacked, stacked], 0, 1, after=[mark])(weight)

    half = jax.ShapeDtypeStruct((ROWS // 2, LANES), F32)
    output, grad, kept, sent, low_edge, high_edge, mark = call(
        functools.partial(forward_kernel, side=side),
        [field, field, half, half, rows, rows],
        4,
        5,
        [
            table,
            columns,
            pltpu.VMEM((3 * channels, 20 * LANES), BF),
            carry_ref,
            pltpu.VMEM((3 * channels, 9 * channels), F32),
            pltpu.VMEM((ROWS, LANES), F32),
            pltpu.VMEM(field.shape, BF),
            sems,
        ],
        2 * flops,
        n_any=2,
        room=20,
    )(
        cells, links, count, bit_of_me(sum_bits()[0][0]),
        below_x, above_x, below_y, above_y, matrix, prepared, upstream,
    )

    halos = [passed_along(high_edge, "gx", 1), passed_along(low_edge, "gx", -1)]
    parts = []
    done = {}

    def columns_task(mark):
        low_column, high_column, mark = call(
            make_columns, [column, column], 1, 3, after=[mark]
        )(cells, grad, *halos)
        halos.append(from_behind(high_column, "gy", 1))
        halos.append(from_behind(low_column, "gy", -1))
        return mark

    def output_task(mark):
        done["output"], mark = call(native_kernel, [native], 0, 1, after=[mark])(output)
        return mark

    def backward_task(group, mark):
        part, mark = call(
            functools.partial(backward_kernel, side=side, group=group),
            [jax.ShapeDtypeStruct((2, 8, channels, LANES), BF)],
            2,
            5,
            [table, columns, carry_ref, pltpu.VMEM((2, 8, channels, LANES), BF), sems],
            4 * flops // pairs,
            n_any=2,
            room=12,
            after=[mark],
        )(links, count, *halos, flipped, grad, upstream)
        parts.append(part)
        return mark

    def gradient_task(mark):
        done["grad"], mark = call(native_kernel, [native], 0, len(parts), after=[mark])(*parts)
        return mark

    tasks = [columns_task, output_task]
    tasks += [functools.partial(backward_task, group) for group in range(pairs // 2)]
    tasks += [gradient_task]
    device_total = lax.axis_size("gx") * lax.axis_size("gy")
    scale = 1.0 / math.sqrt(voxels * slots * device_total)
    mine, block, received, after = summed(kept, sent, mark, scale, dict(enumerate(tasks, 1)))
    grad_weight, _ = call(
        functools.partial(unpack_kernel, height=3 * channels, width=9 * channels),
        [jax.ShapeDtypeStruct((channels, 27 * channels), F32)],
        1,
        2,
        [pltpu.VMEM((ROWS, LANES), BF)],
        after=after,
    )(mine, block, received)
    return (done["output"].reshape(feats.shape), done["grad"].reshape(feats.shape), grad_weight)


def solution(mesh):
    placed = (
        P(None, "gx", "gy", None),
        P(None, "gx", "gy", None),
        P(),
        P("gx", "gy"),
        P("gx", "gy", None),
        P("gx", "gy"),
    )
    return jax.shard_map(
        per_device,
        mesh=mesh,
        in_specs=placed,
        out_specs=(P(None, "gx", "gy", None), P(None, "gx", "gy", None), P()),
        check_vma=False,
    )
```

```python
import functools
import math

import jax
import jax.numpy as jnp
from jax import lax
from jax.experimental import pallas as pl
from jax.experimental.pallas import tpu as pltpu
from jax.sharding import PartitionSpec as P

BF = jnp.bfloat16
F32 = jnp.float32
VMEM = pl.BlockSpec(memory_space=pltpu.VMEM)
SMEM = pl.BlockSpec(memory_space=pltpu.SMEM)
ANY = pl.BlockSpec(memory_space=pl.ANY)
LANES = 128
HALF = 64
ROWS = 2048
GROUPS = 2


def passed_along(block, axis, distance):
    devices = range(lax.axis_size(axis))
    route = [((i - distance) % len(devices), i) for i in devices]
    return lax.ppermute(block, axis, route)


def exchanged(first, second, axis):
    devices = range(lax.axis_size(axis))
    inside = [(i, i ^ 1) for i in devices]
    across = [(i, ((i + 1) ^ 1) - 1) for i in devices]
    across = [(i, j) for i, j in across if j in devices]
    return lax.ppermute(first, axis, inside), lax.ppermute(second, axis, across)


def lane_ids(channels):
    return lax.broadcasted_iota(jnp.int32, (channels, LANES), 1)


def turn(value, amount):
    return pltpu.roll(value, amount, 1)


def nothing(value):
    return jnp.zeros_like(value)


def load_pairs(source, target):
    channels, slots, _ = source.shape
    low = lane_ids(channels) < HALF
    for tile in range(4):
        rows = jnp.swapaxes(source[:, :, tile * LANES : (tile + 1) * LANES], 0, 1)
        for pair in range(slots // 2):
            first, second = rows[2 * pair], rows[2 * pair + 1]
            target[pair, 2 * tile] = jnp.where(low, first, turn(second, HALF))
            target[pair, 2 * tile + 1] = jnp.where(low, turn(first, HALF), second)


def edge_rows(cells, field, low_out, high_out, slots, side):
    channels = field.shape[2]
    low = lane_ids(channels) < HALF
    for out, line, layer in ((low_out, 0, 0), (high_out, side - 1, 7)):
        for tile in range(side // 2):
            parts = []
            for part in range(2):
                slot = cells[line * side + 2 * tile + part]
                row = field[jnp.minimum(slot, slots - 1) // 2, layer]
                row = turn(row, (part + slot) % 2 * HALF)
                parts.append(jnp.where(slot < slots, row, nothing(row)))
            out[tile] = jnp.where(low, parts[0], parts[1])


def prepare_kernel(cells, feats, pairs, low_out, high_out, *, side):
    load_pairs(feats, pairs)
    edge_rows(cells, pairs, low_out, high_out, feats.shape[1], side)


def regroup_kernel(source, pairs):
    load_pairs(source, pairs)


def weights_kernel(weight, matrix, flipped):
    channels = weight.shape[0]
    width = 9 * channels
    for a in range(3):
        rows = slice(a * channels, (a + 1) * channels)
        matrix[rows, :] = weight[:, a * width : (a + 1) * width]
        blocks = []
        for bc in range(9):
            tap = 26 - (a * 9 + bc)
            blocks.append(weight[:, tap * channels : (tap + 1) * channels].T)
        flipped[rows, :] = jnp.concatenate(blocks, axis=1)


def column_kernel(cells, odd, field, below, above, inside, across, *, side):
    channels = field.shape[2]
    slots = 2 * field.shape[0]
    lanes = lane_ids(channels)
    for quarter in range(4):
        both = []
        for line, place in ((0, 0), (side - 1, 56)):
            corner = line % 2 * HALF + place
            total = jnp.zeros((channels, LANES), BF)
            for half in range(2):
                layer = quarter + 4 * half
                for u in range(1, side + 1):
                    slot = cells[(u - 1) * side + line]
                    row = field[jnp.minimum(slot, slots - 1) // 2, layer]
                    goal = half * HALF + u * 8
                    row = turn(row, (goal - place + LANES - slot % 2 * HALF) % LANES)
                    row = jnp.where(slot < slots, row, nothing(row))
                    total = jnp.where(lanes // 8 == goal // 8, row, total)
                if layer == 7:
                    goal = half * HALF
                    row = turn(below[line // 2], (goal - corner) % LANES)
                    total = jnp.where(lanes // 8 == goal // 8, row, total)
                if layer == 0:
                    goal = half * HALF + (side + 1) * 8
                    row = turn(above[line // 2], (goal - corner) % LANES)
                    total = jnp.where(lanes // 8 == goal // 8, row, total)
            both.append(total)
        inside[quarter] = jnp.where(odd[0] == 1, both[0], both[1])
        across[quarter] = jnp.where(odd[0] == 1, both[1], both[0])


def fill_table(table, field, below_x, above_x, inside, across, odd, sem):
    pairs, _, channels, _ = field.shape
    low = lane_ids(channels) < HALF
    copy = pltpu.make_async_copy(field, table.at[pl.ds(0, pairs)], sem)
    copy.start()
    for quarter in range(4):
        below = jnp.where(odd[0] == 1, inside[quarter], across[quarter])
        above = jnp.where(odd[0] == 1, across[quarter], inside[quarter])
        table[pairs, quarter] = jnp.where(low, below, turn(above, HALF))
        table[pairs, quarter + 4] = jnp.where(low, turn(below, HALF), above)
    tiles = below_x.shape[0]
    for tile in range(tiles):
        table[pairs + 1 + tile, 7] = below_x[tile]
        table[pairs + 1 + tile, 0] = above_x[tile]
    table[pairs + 1 + tiles] = jnp.zeros(table.shape[1:], BF)
    copy.wait()


def locate(index, pairs, side, column):
    slots = 2 * pairs
    tiles = side // 2
    wide = side + 2
    place = 0 if column is None else column * 8
    own = index < slots
    row = index < slots + 2 * side
    below = index < slots + side
    ordinal = jnp.where(own, index, index - slots - jnp.where(below, 0, side))
    base = jnp.where(own, 0, pairs + 1)
    tile_row = base + ordinal // 2
    lane_row = ordinal % 2 * HALF + place
    last = index >= slots + 2 * side + 2 * wide
    u = index - slots - 2 * side
    lane_column = jnp.where(u < wide, u * 8, HALF + (u - wide) * 8)
    tile = jnp.where(row, tile_row, jnp.where(last, pairs + 1 + tiles, pairs))
    lane = jnp.where(row, lane_row, jnp.where(last, 0, lane_column))
    return tile, lane


def column_builder(group, links, table, columns, pairs, side):
    channels = table.shape[2]
    lanes = lane_ids(channels)
    low = lanes < HALF
    y_first = lanes % HALF < 8
    y_last = lanes % HALF >= 56
    z_first = lanes % 8 == 0
    z_last = lanes % 8 == 7
    spots = {}
    for h in range(2):
        for part in range(2):
            slot = group * 4 + 2 * h + part
            for k, (dx, dy) in enumerate(
                ((-1, -1), (-1, 0), (-1, 1), (0, -1), (0, 1), (1, -1), (1, 0), (1, 1))
            ):
                column = {-1: 7, 0: None, 1: 0}[dy]
                goal = part * HALF + (56 if dy == 1 else 0)
                tile, lane = locate(links[k, slot], pairs, side, column)
                spots[h, part, dx, dy] = tile, (goal + LANES - lane) % LANES

    def fetch(layer, h, dx, dy):
        rows = []
        for part in range(2):
            tile, amount = spots[h, part, dx, dy]
            rows.append(turn(table[tile, layer], amount))
        return jnp.where(low, rows[0], rows[1])

    def layer_of(xp, layer, dx):
        for h in range(2):
            if dx == 0:
                middle = table[group * 2 + h, layer]
            else:
                middle = fetch(layer, h, dx, 0)
            before = jnp.where(y_first, fetch(layer, h, dx, -1), turn(middle, 8))
            after = jnp.where(y_last, fetch(layer, h, dx, 1), turn(middle, LANES - 8))
            at = xp * 2 * LANES + h * LANES
            for b, value in enumerate((before, middle, after)):
                lower = jnp.where(z_first, nothing(value), turn(value, 1))
                upper = jnp.where(z_last, nothing(value), turn(value, LANES - 1))
                for c, shifted in enumerate((lower, value, upper)):
                    start = (b * 3 + c) * channels
                    columns[start : start + channels, at : at + LANES] = shifted

    def build(xp):
        if xp == 0:
            layer_of(0, 7, -1)
        elif xp == 9:
            layer_of(9, 0, 1)
        else:
            layer_of(xp, xp - 1, 0)

    return build


def product(left, right, contract):
    return lax.dot_general(left, right, (contract, ((), ())), preferred_element_type=F32)


def convolve_group(matrix, columns, carry_ref, build, finish):
    channels = matrix.shape[0] // 3
    width = 2 * LANES
    build(0)
    build(1)
    for step in range(5):
        if step < 4:
            build(2 * step + 2)
            build(2 * step + 3)
        part = product(
            matrix[...], columns[:, step * 2 * width : (step + 1) * 2 * width], ((1,), (0,))
        )
        first, second, third = (part[a * channels : (a + 1) * channels] for a in range(3))
        if step > 0:
            left = carry_ref[:, :width] + third[:, :width]
            right = carry_ref[:, width:] + (second[:, :width] + third[:, width:])
            finish(step - 1, left, right)
        if step < 4:
            carry_ref[:, :width] = first[:, :width] + second[:, width:]
            carry_ref[:, width:] = first[:, width:]


def forward_kernel(
    cells, links, counts, odd, below_x, above_x, inside, across, matrix, field, given,
    out, grad, kept, sent, low_out, high_out,
    table, columns, shifted, carry_ref, total, terms, upstream, sems, *, side,
):
    pairs, _, channels, _ = field.shape
    slots = 2 * pairs
    copy = pltpu.make_async_copy(given, upstream, sems.at[1])
    copy.start()
    fill_table(table, field, below_x, above_x, inside, across, odd, sems.at[0])
    total[...] = jnp.zeros(total.shape, F32)
    shifted[...] = jnp.zeros(shifted.shape, BF)
    upper = (lane_ids(channels) >= HALF).astype(jnp.int32)
    copy.wait()

    def body(group, carry):
        build = column_builder(group, links, table, columns, pairs, side)

        def finish(t, left, right):
            for h in range(2):
                pair = group * 2 + h
                live = 2 * pair + upper < counts[0]
                for odd, hidden in ((0, left), (1, right)):
                    x = 2 * t + odd
                    hidden = hidden[:, h * LANES : (h + 1) * LANES]
                    gate = jax.nn.sigmoid(hidden)
                    inputs = table[pair, x].astype(F32)
                    gradient = upstream[pair, x].astype(F32)
                    result = jnp.where(live, inputs + hidden * gate, 0.0)
                    out[pair, x] = result.astype(BF)
                    gradient = gradient * gate * (1.0 + hidden * (1.0 - gate))
                    gradient = jnp.where(live, gradient, 0.0).astype(BF)
                    grad[pair, x] = gradient
                    for a in range(3):
                        at = (x + a) * 2 * LANES + h * LANES
                        shifted[a * channels : (a + 1) * channels, at : at + LANES] = gradient
            gather_terms(t)

        def gather_terms(step):
            span = slice(step * 4 * LANES, (step + 1) * 4 * LANES)
            total[...] += product(shifted[:, span], columns[:, span], ((1,), (1,)))

        convolve_group(matrix, columns, carry_ref, build, finish)
        gather_terms(4)
        return carry

    lax.fori_loop(0, pairs // 2, body, 0, unroll=True)
    height, width = total.shape
    terms[...] = jnp.zeros(terms.shape, F32)
    for tile in range(-(-width // LANES)):
        end = min(width, (tile + 1) * LANES)
        terms[tile * height : (tile + 1) * height, : end - tile * LANES] = total[
            :, tile * LANES : end
        ]
    half = kept.shape[0]
    kept[...] = terms[pl.ds(pl.multiple_of(odd[0] * half, half), half), :]
    sent[...] = terms[pl.ds(pl.multiple_of((1 - odd[0]) * half, half), half), :]
    edge_rows(cells, grad, low_out, high_out, slots, side)


def backward_kernel(
    links, counts, odd, below_x, above_x, inside, across, matrix, field, given,
    out, table, columns, carry_ref, upstream, sems, *, side, first,
):
    pairs, _, channels, _ = field.shape
    copy = pltpu.make_async_copy(given.at[pl.ds(2 * first, out.shape[0])], upstream, sems.at[1])
    copy.start()
    fill_table(table, field, below_x, above_x, inside, across, odd, sems.at[0])
    upper = (lane_ids(channels) >= HALF).astype(jnp.int32)
    copy.wait()

    def body(index, carry):
        group = first + index
        build = column_builder(group, links, table, columns, pairs, side)

        def finish(t, left, right):
            for h in range(2):
                pair = 2 * index + h
                live = 2 * (group * 2 + h) + upper < counts[0]
                for x, back in ((2 * t, left), (2 * t + 1, right)):
                    gradient = upstream[pair, x].astype(F32) + back[:, h * LANES : (h + 1) * LANES]
                    out[pair, x] = jnp.where(live, gradient, 0.0).astype(BF)

        convolve_group(matrix, columns, carry_ref, build, finish)
        return carry

    lax.fori_loop(0, out.shape[0] // 2, body, 0, unroll=True)


def native_kernel(*refs):
    *parts, out = refs
    low = lane_ids(out.shape[0]) < HALF
    for t in range(4):
        rows = []
        for part in parts:
            for pair in range(part.shape[0]):
                even, odd = part[pair, 2 * t], part[pair, 2 * t + 1]
                rows.append(jnp.where(low, even, turn(odd, HALF)))
                rows.append(jnp.where(low, turn(even, HALF), odd))
        out[:, :, t * LANES : (t + 1) * LANES] = jnp.swapaxes(jnp.stack(rows), 0, 1)


def unpack_kernel(mine, block, received, out, joined, *, height, width):
    join_kernel(mine, block, received, joined)
    channels = out.shape[0]
    tiles = -(-width // LANES)
    blocks = []
    for a in range(height // channels):
        for tile in range(tiles):
            start = tile * height + a * channels
            piece = joined[start : start + channels, :].astype(F32)
            blocks.append(piece[:, : min(LANES, width - tile * LANES)])
    out[...] = jnp.concatenate(blocks, axis=1)


def call(kernel, out_shape, n_smem, n_vmem, scratch=(), flops=0, n_any=0, room=10, after=()):
    inputs, outputs = n_smem + n_vmem + n_any, len(out_shape)

    def body(*refs):
        refs, marks = refs[:inputs], refs[inputs + len(after) :]
        kernel(*refs, *marks[:outputs], *marks[outputs + 1 :])
        marks[outputs][...] = jnp.zeros((8, LANES), F32)

    called = pl.pallas_call(
        body,
        out_shape=[*out_shape, jax.ShapeDtypeStruct((8, LANES), F32)],
        in_specs=[SMEM] * n_smem + [VMEM] * n_vmem + [ANY] * (n_any + len(after)),
        out_specs=[VMEM] * (outputs + 1),
        scratch_shapes=list(scratch),
        compiler_params=pltpu.CompilerParams(vmem_limit_bytes=room << 20),
        cost_estimate=pl.CostEstimate(flops=flops, bytes_accessed=4 << 20, transcendentals=0),
    )
    return lambda *args: called(*args, *after)


def split_kernel(mine, kept, received, kept_out, sent_out):
    half = kept_out.shape[0]
    here = pl.multiple_of(mine[0] * half, half)
    there = pl.multiple_of((1 - mine[0]) * half, half)
    kept_out[...] = kept[pl.ds(here, half), :] + received[pl.ds(here, half), :]
    sent_out[...] = kept[pl.ds(there, half), :] + received[pl.ds(there, half), :]


def add_kernel(kept, received, out, *, scale):
    total = kept[...] + received[...]
    out[...] = total if scale is None else (total * scale).astype(BF)


def join_kernel(mine, block, received, out):
    half = block.shape[0]
    out[pl.ds(pl.multiple_of(mine[0] * half, half), half), :] = block[...]
    out[pl.ds(pl.multiple_of((1 - mine[0]) * half, half), half), :] = received[...]


def sum_bits():
    devices = lax.axis_size("gx") * lax.axis_size("gy")
    bits = [1 << b for b in range(devices.bit_length() - 1)]
    inner = [bit for bit in bits if bit < lax.axis_size("gy")]
    return inner, bits[len(inner) :]


def bit_of_me(bit):
    me = lax.axis_index("gx") * lax.axis_size("gy") + lax.axis_index("gy")
    return (me // bit % 2).reshape(1)


def summed(kept, sent, mark, scale, tasks):
    axes = ("gx", "gy")
    devices = lax.axis_size("gx") * lax.axis_size("gy")
    inner, outer = sum_bits()

    def swapped(block, bit):
        return lax.ppermute(block, axes, [(i, i ^ bit) for i in range(devices)])

    def like(block, factor, kind=F32):
        return jax.ShapeDtypeStruct((int(block.shape[0] * factor), LANES), kind)

    order = inner + outer + inner[::-1]
    block = kept
    for step, bit in enumerate(order):
        received = swapped(sent if step < len(inner) else block, bit)
        after = [tasks[step](mark)] if step in tasks else []
        if step + 1 < len(inner):
            half = like(block, 0.5)
            block, sent, _ = call(split_kernel, [half, half], 1, 2, after=after)(
                bit_of_me(order[step + 1]), block, received
            )
            mark = sent
        elif step < len(inner) + len(outer):
            last = step + 1 == len(inner) + len(outer)
            kernel = functools.partial(add_kernel, scale=scale if last else None)
            block, mark = call(kernel, [like(block, 1, BF if last else F32)], 0, 2, after=after)(
                block, received
            )
        elif step + 1 < len(order):
            block, mark = call(join_kernel, [like(block, 2, BF)], 1, 2, after=after)(
                bit_of_me(bit), block, received
            )
        else:
            return bit_of_me(bit), block, received, after


def per_device(feats, cotangent, weight, cell_slot, neighbours, counts):
    channels, _, slots, voxels = feats.shape
    side = math.isqrt(cell_slot.shape[1])
    pairs = slots // 2
    cells = cell_slot.reshape(side * side)
    links = neighbours.reshape(slots, 8).T
    count = counts.reshape(1)
    native = jax.ShapeDtypeStruct((channels, slots, voxels), BF)
    field = jax.ShapeDtypeStruct((pairs, 8, channels, LANES), BF)
    rows = jax.ShapeDtypeStruct((side // 2, channels, LANES), BF)
    column = jax.ShapeDtypeStruct((4, channels, LANES), BF)
    table = pltpu.VMEM((pairs + 2 + side // 2, 8, channels, LANES), BF)
    columns = pltpu.VMEM((9 * channels, 20 * LANES), BF)
    carry_ref = pltpu.VMEM((channels, 4 * LANES), F32)
    sems = pltpu.SemaphoreType.DMA((2,))
    flops = 2 * 27 * channels * channels * slots * voxels

    prepared, low_edge, high_edge, _ = call(
        functools.partial(prepare_kernel, side=side), [field, rows, rows], 1, 1
    )(cells, feats.reshape(channels, slots, voxels))
    below_x = passed_along(high_edge, "gx", 1)
    above_x = passed_along(low_edge, "gx", -1)
    upstream, mark = call(regroup_kernel, [field], 0, 1)(
        cotangent.reshape(channels, slots, voxels)
    )
    make_columns = functools.partial(column_kernel, side=side)
    odd = (lax.axis_index("gy") % 2).reshape(1)
    *both, mark = call(make_columns, [column, column], 2, 3, after=[mark])(
        cells, odd, prepared, below_x, above_x
    )
    inside, across = exchanged(*both, "gy")
    stacked = jax.ShapeDtypeStruct((3 * channels, 9 * channels), BF)
    matrix, flipped, _ = call(weights_kernel, [stacked, stacked], 0, 1, after=[mark])(weight)

    half = jax.ShapeDtypeStruct((ROWS // 2, LANES), F32)
    output, grad, kept, sent, low_edge, high_edge, mark = call(
        functools.partial(forward_kernel, side=side),
        [field, field, half, half, rows, rows],
        4,
        5,
        [
            table,
            columns,
            pltpu.VMEM((3 * channels, 20 * LANES), BF),
            carry_ref,
            pltpu.VMEM((3 * channels, 9 * channels), F32),
            pltpu.VMEM((ROWS, LANES), F32),
            pltpu.VMEM(field.shape, BF),
            sems,
        ],
        2 * flops,
        n_any=2,
        room=20,
    )(
        cells, links, count, odd, below_x, above_x, inside, across, matrix, prepared, upstream,
    )

    halos = [passed_along(high_edge, "gx", 1), passed_along(low_edge, "gx", -1)]
    parts = []
    done = {}

    def columns_task(mark):
        *both, mark = call(make_columns, [column, column], 2, 3, after=[mark])(
            cells, odd, grad, *halos
        )
        halos.extend(exchanged(*both, "gy"))
        return mark

    def output_task(mark):
        done["output"], mark = call(native_kernel, [native], 0, 1, after=[mark])(output)
        return mark

    def backward_task(first, mark):
        part, mark = call(
            functools.partial(backward_kernel, side=side, first=first),
            [jax.ShapeDtypeStruct((2 * GROUPS, 8, channels, LANES), BF)],
            3,
            5,
            [table, columns, carry_ref, pltpu.VMEM((2 * GROUPS, 8, channels, LANES), BF), sems],
            2 * GROUPS * flops // pairs,
            n_any=2,
            room=12,
            after=[mark],
        )(links, count, odd, *halos, flipped, grad, upstream)
        parts.append(part)
        return mark

    def gradient_task(mark):
        done["grad"], mark = call(native_kernel, [native], 0, len(parts), after=[mark])(*parts)
        return mark

    tasks = [columns_task, output_task]
    tasks += [functools.partial(backward_task, group) for group in range(0, pairs // 2, GROUPS)]
    tasks += [gradient_task]
    device_total = lax.axis_size("gx") * lax.axis_size("gy")
    scale = 1.0 / math.sqrt(voxels * slots * device_total)
    mine, block, received, after = summed(kept, sent, mark, scale, dict(enumerate(tasks, 1)))
    grad_weight, _ = call(
        functools.partial(unpack_kernel, height=3 * channels, width=9 * channels),
        [jax.ShapeDtypeStruct((channels, 27 * channels), F32)],
        1,
        2,
        [pltpu.VMEM((ROWS, LANES), BF)],
        after=after,
    )(mine, block, received)
    return (done["output"].reshape(feats.shape), done["grad"].reshape(feats.shape), grad_weight)


def solution(mesh):
    placed = (
        P(None, "gx", "gy", None),
        P(None, "gx", "gy", None),
        P(),
        P("gx", "gy"),
        P("gx", "gy", None),
        P("gx", "gy"),
    )
    return jax.shard_map(
        per_device,
        mesh=mesh,
        in_specs=placed,
        out_specs=(P(None, "gx", "gy", None), P(None, "gx", "gy", None), P()),
        check_vma=False,
    )
```

```python
import functools
import math

import jax
import jax.numpy as jnp
from jax import lax
from jax.experimental import pallas as pl
from jax.experimental.pallas import tpu as pltpu
from jax.sharding import PartitionSpec as P

BF = jnp.bfloat16
F32 = jnp.float32
VMEM = pl.BlockSpec(memory_space=pltpu.VMEM)
SMEM = pl.BlockSpec(memory_space=pltpu.SMEM)
ANY = pl.BlockSpec(memory_space=pl.ANY)
LANES = 128
HALF = 64
ROWS = 2048
GROUPS = 2


def passed_along(block, axis, distance):
    devices = range(lax.axis_size(axis))
    route = [((i - distance) % len(devices), i) for i in devices]
    return lax.ppermute(block, axis, route)


def exchanged(first, second, axis):
    devices = range(lax.axis_size(axis))
    inside = [(i, i ^ 1) for i in devices]
    across = [(i, ((i + 1) ^ 1) - 1) for i in devices]
    across = [(i, j) for i, j in across if j in devices]
    return lax.ppermute(first, axis, inside), lax.ppermute(second, axis, across)


def lane_ids(channels):
    return lax.broadcasted_iota(jnp.int32, (channels, LANES), 1)


def turn(value, amount):
    return pltpu.roll(value, amount, 1)


def nothing(value):
    return jnp.zeros_like(value)


def load_pairs(source, target):
    channels, slots, _ = source.shape
    low = lane_ids(channels) < HALF
    for tile in range(4):
        rows = jnp.swapaxes(source[:, :, tile * LANES : (tile + 1) * LANES], 0, 1)
        for pair in range(slots // 2):
            first, second = rows[2 * pair], rows[2 * pair + 1]
            target[pair, 2 * tile] = jnp.where(low, first, turn(second, HALF))
            target[pair, 2 * tile + 1] = jnp.where(low, turn(first, HALF), second)


def edge_rows(cells, field, low_out, high_out, slots, side):
    channels = field.shape[2]
    low = lane_ids(channels) < HALF
    for out, line, layer in ((low_out, 0, 0), (high_out, side - 1, 7)):
        for tile in range(side // 2):
            parts = []
            for part in range(2):
                slot = cells[line * side + 2 * tile + part]
                row = field[jnp.minimum(slot, slots - 1) // 2, layer]
                row = turn(row, (part + slot) % 2 * HALF)
                parts.append(jnp.where(slot < slots, row, nothing(row)))
            out[tile] = jnp.where(low, parts[0], parts[1])


def prepare_kernel(cells, feats, pairs, low_out, high_out, *, side):
    load_pairs(feats, pairs)
    edge_rows(cells, pairs, low_out, high_out, feats.shape[1], side)


def regroup_kernel(source, pairs):
    load_pairs(source, pairs)


def weights_kernel(weight, matrix, flipped):
    channels = weight.shape[0]
    width = 9 * channels
    for a in range(3):
        rows = slice(a * channels, (a + 1) * channels)
        matrix[rows, :] = weight[:, a * width : (a + 1) * width]
        blocks = []
        for bc in range(9):
            tap = 26 - (a * 9 + bc)
            blocks.append(weight[:, tap * channels : (tap + 1) * channels].T)
        flipped[rows, :] = jnp.concatenate(blocks, axis=1)


def column_kernel(cells, odd, field, below, above, inside, across, *, side):
    channels = field.shape[2]
    slots = 2 * field.shape[0]
    lanes = lane_ids(channels)
    for quarter in range(4):
        both = []
        for line, place in ((0, 0), (side - 1, 56)):
            corner = line % 2 * HALF + place
            total = jnp.zeros((channels, LANES), BF)
            for half in range(2):
                layer = quarter + 4 * half
                for u in range(1, side + 1):
                    slot = cells[(u - 1) * side + line]
                    row = field[jnp.minimum(slot, slots - 1) // 2, layer]
                    goal = half * HALF + u * 8
                    row = turn(row, (goal - place + LANES - slot % 2 * HALF) % LANES)
                    row = jnp.where(slot < slots, row, nothing(row))
                    total = jnp.where(lanes // 8 == goal // 8, row, total)
                if layer == 7:
                    goal = half * HALF
                    row = turn(below[line // 2], (goal - corner) % LANES)
                    total = jnp.where(lanes // 8 == goal // 8, row, total)
                if layer == 0:
                    goal = half * HALF + (side + 1) * 8
                    row = turn(above[line // 2], (goal - corner) % LANES)
                    total = jnp.where(lanes // 8 == goal // 8, row, total)
            both.append(total)
        inside[quarter] = jnp.where(odd[0] == 1, both[0], both[1])
        across[quarter] = jnp.where(odd[0] == 1, both[1], both[0])


def fill_table(table, field, below_x, above_x, inside, across, odd, sem):
    pairs, _, channels, _ = field.shape
    low = lane_ids(channels) < HALF
    copy = pltpu.make_async_copy(field, table.at[pl.ds(0, pairs)], sem)
    copy.start()
    for quarter in range(4):
        below = jnp.where(odd[0] == 1, inside[quarter], across[quarter])
        above = jnp.where(odd[0] == 1, across[quarter], inside[quarter])
        table[pairs, quarter] = jnp.where(low, below, turn(above, HALF))
        table[pairs, quarter + 4] = jnp.where(low, turn(below, HALF), above)
    tiles = below_x.shape[0]
    for tile in range(tiles):
        table[pairs + 1 + tile, 7] = below_x[tile]
        table[pairs + 1 + tile, 0] = above_x[tile]
    table[pairs + 1 + tiles] = jnp.zeros(table.shape[1:], BF)
    copy.wait()


def locate(index, pairs, side, column):
    slots = 2 * pairs
    tiles = side // 2
    wide = side + 2
    place = 0 if column is None else column * 8
    own = index < slots
    row = index < slots + 2 * side
    below = index < slots + side
    ordinal = jnp.where(own, index, index - slots - jnp.where(below, 0, side))
    base = jnp.where(own, 0, pairs + 1)
    tile_row = base + ordinal // 2
    lane_row = ordinal % 2 * HALF + place
    last = index >= slots + 2 * side + 2 * wide
    u = index - slots - 2 * side
    lane_column = jnp.where(u < wide, u * 8, HALF + (u - wide) * 8)
    tile = jnp.where(row, tile_row, jnp.where(last, pairs + 1 + tiles, pairs))
    lane = jnp.where(row, lane_row, jnp.where(last, 0, lane_column))
    return tile, lane


def column_builder(group, links, table, columns, pairs, side):
    channels = table.shape[2]
    lanes = lane_ids(channels)
    low = lanes < HALF
    y_first = lanes % HALF < 8
    y_last = lanes % HALF >= 56
    z_first = lanes % 8 == 0
    z_last = lanes % 8 == 7
    spots = {}
    for h in range(2):
        for part in range(2):
            slot = group * 4 + 2 * h + part
            for k, (dx, dy) in enumerate(
                ((-1, -1), (-1, 0), (-1, 1), (0, -1), (0, 1), (1, -1), (1, 0), (1, 1))
            ):
                column = {-1: 7, 0: None, 1: 0}[dy]
                goal = part * HALF + (56 if dy == 1 else 0)
                tile, lane = locate(links[k, slot], pairs, side, column)
                spots[h, part, dx, dy] = tile, (goal + LANES - lane) % LANES

    def fetch(layer, h, dx, dy):
        rows = []
        for part in range(2):
            tile, amount = spots[h, part, dx, dy]
            rows.append(turn(table[tile, layer], amount))
        return jnp.where(low, rows[0], rows[1])

    def layer_of(xp, layer, dx):
        for h in range(2):
            if dx == 0:
                middle = table[group * 2 + h, layer]
            else:
                middle = fetch(layer, h, dx, 0)
            before = jnp.where(y_first, fetch(layer, h, dx, -1), turn(middle, 8))
            after = jnp.where(y_last, fetch(layer, h, dx, 1), turn(middle, LANES - 8))
            at = xp * 2 * LANES + h * LANES
            for b, value in enumerate((before, middle, after)):
                lower = jnp.where(z_first, nothing(value), turn(value, 1))
                upper = jnp.where(z_last, nothing(value), turn(value, LANES - 1))
                for c, shifted in enumerate((lower, value, upper)):
                    start = (b * 3 + c) * channels
                    columns[start : start + channels, at : at + LANES] = shifted

    def build(xp):
        if xp == 0:
            layer_of(0, 7, -1)
        elif xp == 9:
            layer_of(9, 0, 1)
        else:
            layer_of(xp, xp - 1, 0)

    return build


def product(left, right, contract):
    return lax.dot_general(left, right, (contract, ((), ())), preferred_element_type=F32)


def convolve_group(matrix, columns, carry_ref, build, finish):
    channels = matrix.shape[0] // 3
    width = 2 * LANES
    build(0)
    build(1)
    for step in range(5):
        if step < 4:
            build(2 * step + 2)
            build(2 * step + 3)
        part = product(
            matrix[...], columns[:, step * 2 * width : (step + 1) * 2 * width], ((1,), (0,))
        )
        first, second, third = (part[a * channels : (a + 1) * channels] for a in range(3))
        if step > 0:
            left = carry_ref[:, :width] + third[:, :width]
            right = carry_ref[:, width:] + (second[:, :width] + third[:, width:])
            finish(step - 1, left, right)
        if step < 4:
            carry_ref[:, :width] = first[:, :width] + second[:, width:]
            carry_ref[:, width:] = first[:, width:]


def forward_kernel(
    cells, links, counts, odd, below_x, above_x, inside, across, matrix, field, given,
    out, grad, kept, sent, low_out, high_out,
    table, columns, shifted, carry_ref, total, terms, upstream, sems, *, side,
):
    pairs, _, channels, _ = field.shape
    slots = 2 * pairs
    copy = pltpu.make_async_copy(given, upstream, sems.at[1])
    copy.start()
    fill_table(table, field, below_x, above_x, inside, across, odd, sems.at[0])
    total[...] = jnp.zeros(total.shape, F32)
    shifted[...] = jnp.zeros(shifted.shape, BF)
    upper = (lane_ids(channels) >= HALF).astype(jnp.int32)
    copy.wait()

    def body(group, carry):
        build = column_builder(group, links, table, columns, pairs, side)

        def finish(t, left, right):
            for h in range(2):
                pair = group * 2 + h
                live = 2 * pair + upper < counts[0]
                for odd, hidden in ((0, left), (1, right)):
                    x = 2 * t + odd
                    hidden = hidden[:, h * LANES : (h + 1) * LANES]
                    gate = jax.nn.sigmoid(hidden)
                    inputs = table[pair, x].astype(F32)
                    gradient = upstream[pair, x].astype(F32)
                    result = jnp.where(live, inputs + hidden * gate, 0.0)
                    out[pair, x] = result.astype(BF)
                    gradient = gradient * gate * (1.0 + hidden * (1.0 - gate))
                    gradient = jnp.where(live, gradient, 0.0).astype(BF)
                    grad[pair, x] = gradient
                    for a in range(3):
                        at = (x + a) * 2 * LANES + h * LANES
                        shifted[a * channels : (a + 1) * channels, at : at + LANES] = gradient
            gather_terms(t)

        def gather_terms(step):
            span = slice(step * 4 * LANES, (step + 1) * 4 * LANES)
            total[...] += product(shifted[:, span], columns[:, span], ((1,), (1,)))

        convolve_group(matrix, columns, carry_ref, build, finish)
        gather_terms(4)
        return carry

    lax.fori_loop(0, pairs // 2, body, 0, unroll=True)
    height, width = total.shape
    terms[...] = jnp.zeros(terms.shape, F32)
    for tile in range(-(-width // LANES)):
        end = min(width, (tile + 1) * LANES)
        terms[tile * height : (tile + 1) * height, : end - tile * LANES] = total[
            :, tile * LANES : end
        ]
    half = kept.shape[0]
    kept[...] = terms[pl.ds(pl.multiple_of(odd[0] * half, half), half), :]
    sent[...] = terms[pl.ds(pl.multiple_of((1 - odd[0]) * half, half), half), :]
    edge_rows(cells, grad, low_out, high_out, slots, side)


def backward_kernel(
    links, counts, odd, below_x, above_x, inside, across, matrix, field, given,
    out, table, columns, carry_ref, upstream, sems, *, side, first,
):
    pairs, _, channels, _ = field.shape
    copy = pltpu.make_async_copy(given.at[pl.ds(2 * first, out.shape[0])], upstream, sems.at[1])
    copy.start()
    fill_table(table, field, below_x, above_x, inside, across, odd, sems.at[0])
    upper = (lane_ids(channels) >= HALF).astype(jnp.int32)
    copy.wait()

    def body(index, carry):
        group = first + index
        build = column_builder(group, links, table, columns, pairs, side)

        def finish(t, left, right):
            for h in range(2):
                pair = 2 * index + h
                live = 2 * (group * 2 + h) + upper < counts[0]
                for x, back in ((2 * t, left), (2 * t + 1, right)):
                    gradient = upstream[pair, x].astype(F32) + back[:, h * LANES : (h + 1) * LANES]
                    out[pair, x] = jnp.where(live, gradient, 0.0).astype(BF)

        convolve_group(matrix, columns, carry_ref, build, finish)
        return carry

    lax.fori_loop(0, out.shape[0] // 2, body, 0, unroll=True)


def native_kernel(*refs):
    *parts, out = refs
    low = lane_ids(out.shape[0]) < HALF
    for t in range(4):
        rows = []
        for part in parts:
            for pair in range(part.shape[0]):
                even, odd = part[pair, 2 * t], part[pair, 2 * t + 1]
                rows.append(jnp.where(low, even, turn(odd, HALF)))
                rows.append(jnp.where(low, turn(even, HALF), odd))
        out[:, :, t * LANES : (t + 1) * LANES] = jnp.swapaxes(jnp.stack(rows), 0, 1)


def unpack_kernel(mine, block, received, out, joined, *, height, width):
    join_kernel(mine, block, received, joined)
    channels = out.shape[0]
    tiles = -(-width // LANES)
    blocks = []
    for a in range(height // channels):
        for tile in range(tiles):
            start = tile * height + a * channels
            piece = joined[start : start + channels, :].astype(F32)
            blocks.append(piece[:, : min(LANES, width - tile * LANES)])
    out[...] = jnp.concatenate(blocks, axis=1)


def call(kernel, out_shape, n_smem, n_vmem, scratch=(), flops=0, n_any=0, room=10, after=()):
    inputs, outputs = n_smem + n_vmem + n_any, len(out_shape)

    def body(*refs):
        refs, marks = refs[:inputs], refs[inputs + len(after) :]
        kernel(*refs, *marks[:outputs], *marks[outputs + 1 :])
        marks[outputs][...] = jnp.zeros((8, LANES), F32)

    called = pl.pallas_call(
        body,
        out_shape=[*out_shape, jax.ShapeDtypeStruct((8, LANES), F32)],
        in_specs=[SMEM] * n_smem + [VMEM] * n_vmem + [ANY] * (n_any + len(after)),
        out_specs=[VMEM] * (outputs + 1),
        scratch_shapes=list(scratch),
        compiler_params=pltpu.CompilerParams(vmem_limit_bytes=room << 20),
        cost_estimate=pl.CostEstimate(flops=flops, bytes_accessed=4 << 20, transcendentals=0),
    )
    return lambda *args: called(*args, *after)


def split_kernel(mine, kept, received, kept_out, sent_out):
    half = kept_out.shape[0]
    here = pl.multiple_of(mine[0] * half, half)
    there = pl.multiple_of((1 - mine[0]) * half, half)
    kept_out[...] = kept[pl.ds(here, half), :] + received[pl.ds(here, half), :]
    sent_out[...] = kept[pl.ds(there, half), :] + received[pl.ds(there, half), :]


def add_kernel(kept, received, out, *, scale):
    total = kept[...] + received[...]
    out[...] = total if scale is None else (total * scale).astype(BF)


def join_kernel(mine, block, received, out):
    half = block.shape[0]
    out[pl.ds(pl.multiple_of(mine[0] * half, half), half), :] = block[...]
    out[pl.ds(pl.multiple_of((1 - mine[0]) * half, half), half), :] = received[...]


def sum_bits():
    devices = lax.axis_size("gx") * lax.axis_size("gy")
    bits = [1 << b for b in range(devices.bit_length() - 1)]
    inner = [bit for bit in bits if bit < lax.axis_size("gy")]
    return inner, bits[len(inner) :]


def bit_of_me(bit):
    me = lax.axis_index("gx") * lax.axis_size("gy") + lax.axis_index("gy")
    return (me // bit % 2).reshape(1)


def summed(kept, sent, mark, scale, tasks):
    axes = ("gx", "gy")
    devices = lax.axis_size("gx") * lax.axis_size("gy")
    inner, outer = sum_bits()

    def swapped(block, bit):
        return lax.ppermute(block, axes, [(i, i ^ bit) for i in range(devices)])

    def like(block, factor, kind=F32):
        return jax.ShapeDtypeStruct((int(block.shape[0] * factor), LANES), kind)

    order = inner + outer + inner[::-1]
    block = kept
    for step, bit in enumerate(order):
        received = swapped(sent if step < len(inner) else block, bit)
        after = [tasks[step](mark)] if step in tasks else []
        if step + 1 < len(inner):
            half = like(block, 0.5)
            block, sent, _ = call(split_kernel, [half, half], 1, 2, after=after)(
                bit_of_me(order[step + 1]), block, received
            )
            mark = sent
        elif step < len(inner) + len(outer):
            last = step + 1 == len(inner) + len(outer)
            kernel = functools.partial(add_kernel, scale=scale if last else None)
            block, mark = call(kernel, [like(block, 1, BF if last else F32)], 0, 2, after=after)(
                block, received
            )
        elif step + 1 < len(order):
            block, mark = call(join_kernel, [like(block, 2, BF)], 1, 2, after=after)(
                bit_of_me(bit), block, received
            )
        else:
            return bit_of_me(bit), block, received, after


def per_device(feats, cotangent, weight, cell_slot, neighbours, counts):
    channels, _, slots, voxels = feats.shape
    side = math.isqrt(cell_slot.shape[1])
    pairs = slots // 2
    cells = cell_slot.reshape(side * side)
    links = neighbours.reshape(slots, 8).T
    count = counts.reshape(1)
    native = jax.ShapeDtypeStruct((channels, slots, voxels), BF)
    field = jax.ShapeDtypeStruct((pairs, 8, channels, LANES), BF)
    rows = jax.ShapeDtypeStruct((side // 2, channels, LANES), BF)
    column = jax.ShapeDtypeStruct((4, channels, LANES), BF)
    table = pltpu.VMEM((pairs + 2 + side // 2, 8, channels, LANES), BF)
    columns = pltpu.VMEM((9 * channels, 20 * LANES), BF)
    carry_ref = pltpu.VMEM((channels, 4 * LANES), F32)
    sems = pltpu.SemaphoreType.DMA((2,))
    flops = 2 * 27 * channels * channels * slots * voxels

    prepared, low_edge, high_edge, _ = call(
        functools.partial(prepare_kernel, side=side), [field, rows, rows], 1, 1
    )(cells, feats.reshape(channels, slots, voxels))
    below_x = passed_along(high_edge, "gx", 1)
    above_x = passed_along(low_edge, "gx", -1)
    upstream, mark = call(regroup_kernel, [field], 0, 1)(
        cotangent.reshape(channels, slots, voxels)
    )
    make_columns = functools.partial(column_kernel, side=side)
    odd = (lax.axis_index("gy") % 2).reshape(1)
    *both, mark = call(make_columns, [column, column], 2, 3, after=[mark])(
        cells, odd, prepared, below_x, above_x
    )
    inside, across = exchanged(*both, "gy")
    stacked = jax.ShapeDtypeStruct((3 * channels, 9 * channels), BF)
    matrix, flipped, _ = call(weights_kernel, [stacked, stacked], 0, 1, after=[mark])(weight)

    half = jax.ShapeDtypeStruct((ROWS // 2, LANES), F32)
    output, grad, kept, sent, low_edge, high_edge, mark = call(
        functools.partial(forward_kernel, side=side),
        [field, field, half, half, rows, rows],
        4,
        5,
        [
            table,
            columns,
            pltpu.VMEM((3 * channels, 20 * LANES), BF),
            carry_ref,
            pltpu.VMEM((3 * channels, 9 * channels), F32),
            pltpu.VMEM((ROWS, LANES), F32),
            pltpu.VMEM(field.shape, BF),
            sems,
        ],
        2 * flops,
        n_any=2,
        room=20,
    )(
        cells, links, count, odd, below_x, above_x, inside, across, matrix, prepared, upstream,
    )

    halos = [passed_along(high_edge, "gx", 1), passed_along(low_edge, "gx", -1)]
    parts = []
    done = {}

    def columns_task(mark):
        *both, mark = call(make_columns, [column, column], 2, 3, after=[mark])(
            cells, odd, grad, *halos
        )
        halos.extend(exchanged(*both, "gy"))
        return mark

    def output_task(mark):
        done["output"], mark = call(native_kernel, [native], 0, 1, after=[mark])(output)
        return mark

    def backward_task(first, mark):
        part, mark = call(
            functools.partial(backward_kernel, side=side, first=first),
            [jax.ShapeDtypeStruct((2 * GROUPS, 8, channels, LANES), BF)],
            3,
            5,
            [table, columns, carry_ref, pltpu.VMEM((2 * GROUPS, 8, channels, LANES), BF), sems],
            2 * GROUPS * flops // pairs,
            n_any=2,
            room=12,
            after=[mark],
        )(links, count, odd, *halos, flipped, grad, upstream)
        parts.append(part)
        return mark

    def gradient_task(mark):
        done["grad"], mark = call(native_kernel, [native], 0, len(parts), after=[mark])(*parts)
        return mark

    tasks = [columns_task, lambda mark: mark]
    tasks += [functools.partial(backward_task, group) for group in range(0, pairs // 2, GROUPS)]
    tasks += [gradient_task, output_task]
    device_total = lax.axis_size("gx") * lax.axis_size("gy")
    scale = 1.0 / math.sqrt(voxels * slots * device_total)
    mine, block, received, after = summed(kept, sent, mark, scale, dict(enumerate(tasks, 1)))
    grad_weight, _ = call(
        functools.partial(unpack_kernel, height=3 * channels, width=9 * channels),
        [jax.ShapeDtypeStruct((channels, 27 * channels), F32)],
        1,
        2,
        [pltpu.VMEM((ROWS, LANES), BF)],
        after=after,
    )(mine, block, received)
    return (done["output"].reshape(feats.shape), done["grad"].reshape(feats.shape), grad_weight)


def solution(mesh):
    placed = (
        P(None, "gx", "gy", None),
        P(None, "gx", "gy", None),
        P(),
        P("gx", "gy"),
        P("gx", "gy", None),
        P("gx", "gy"),
    )
    return jax.shard_map(
        per_device,
        mesh=mesh,
        in_specs=placed,
        out_specs=(P(None, "gx", "gy", None), P(None, "gx", "gy", None), P()),
        check_vma=False,
    )
```
